256 devices in a mesh: shot: 16 (over y, x_lo, core), slab: 16 (over x_hi, z).
Axes of the slice: x: 4 (x_hi: 2, x_lo: 2; x = x_hi * 2 + x_lo), y: 4, z: 8, core: 2. Of those that a mesh axis runs over, the one named last changes fastest.
Arguments:
- velocity: float32 [256, 64, 128], P('slab', 'shot'), may hold values from 0.2 to 0.42
- fields_prev: float32 [16, 2, 256, 64, 128], P('shot', None, 'slab'), may hold values from -6 to 6
- fields_now: float32 [16, 2, 256, 64, 128], P('shot', None, 'slab'), may hold values from -6 to 6
- source_cells: int32 [16, 32], P('shot', 'slab'), may hold values from 32768 to 98303
- source_traces: float32 [16, 8, 32], P('shot', None, 'slab'), may hold values from -6 to 6
- receiver_cells: int32 [16, 4096], P('shot', 'slab'), may hold values from 32768 to 98303
- receiver_traces: float32 [16, 8, 4096], P('shot', None, 'slab'), may hold values from -6 to 6
Outputs:
- gradient: float32 [256, 64, 128], P('slab', 'shot')
- fields_before: float32 [16, 2, 256, 64, 128], P('shot', None, 'slab')
- fields_after: float32 [16, 2, 256, 64, 128], P('shot', None, 'slab')
The draws below stay inside these ranges and needn't reach their ends.
Inputs may be any that keep to these rules, and one draw needn't show every extreme that they name: `receiver_cells`: block j of each row (entries j * 256 onward) numbers cells of depth slab j, counted from that slab's first plane, plane then first then second lateral index, on planes 4 to 11 of the slab. `source_cells`: block j of each row (entries j * 2 onward) numbers cells of depth slab j, counted from that slab's first plane, plane then first then second lateral index, on planes 4 to 11 of the slab.
All inputs are finite; a program needn't handle non-finite values.
Results may differ from the reference program's by a relative error of at most 0.0003.
Values sent between devices are 32-bit elements; how exact they have to be, the bound alone decides.
No kernel may reach another device: no remote copies, remote signals or barrier semaphores. Data moves between devices by JAX's collectives and lax.ppermute only.
A program may use at most 64 MiB of HBM per device.

```python
import jax
import jax.numpy as jnp
from jax import lax

PLANES = 16
NX = 64
NY = 128
STEPS = 8
SRC_DEV = 2
RECV_DEV = 256
SHOTS = 16
NZ = 256
SRC_TOTAL = 32
RECV_TOTAL = 4096


def wave_field(key, amp_lo, amp_hi):
    keys = jax.random.split(key, 3)
    depth_sign = 1.0 - 2.0 * (jnp.arange(NZ, dtype=jnp.int32) % 2).astype(jnp.float32)
    random_sign = 1.0 - 2.0 * jax.random.randint(keys[0], (SHOTS, 2, 1, NX, NY), 0, 2).astype(jnp.float32)
    column_sign = random_sign
    amplitude = amp_lo + (amp_hi - amp_lo) * jax.random.uniform(keys[1], (SHOTS, 2, NZ, NX, NY), jnp.float32)
    noise = jnp.clip(jax.random.normal(keys[2], (SHOTS, 2, NZ, NX, NY), jnp.float32), -1.5, 1.5)
    return depth_sign[None, None, :, None, None] * column_sign * amplitude + noise


def draw_velocity(key, part):
    key = jax.random.fold_in(key, 11)
    plane = jnp.arange(NZ, dtype=jnp.int32) % PLANES
    border = ((plane < 4) | (plane >= PLANES - 4))[:, None, None]
    pick = jax.random.uniform(key, (NZ, NX, NY), jnp.float32)
    near = 0.33 * jnp.exp(jnp.log(0.42 / 0.33) * pick)
    far = 0.2 * jnp.exp(jnp.log(2.1) * pick)
    return jnp.clip(jnp.where(border, near, far), 0.2, 0.42)


def draw_fields_prev(key, part):
    key = jax.random.fold_in(key, 23)
    return wave_field(key, 2.0, 4.0)


def draw_fields_now(key, part):
    key = jax.random.fold_in(key, 37)
    return wave_field(key, 2.0, 4.0)


def place_ends(values, own_key, least, top_value):
    longest = values.shape.index(max(values.shape))
    spots = []
    for shift in (0, 1):
        where = [jax.random.randint(jax.random.fold_in(own_key, axis), (), 0, length) for axis, length in enumerate(values.shape)]
        where[longest] = (where[longest] + shift) % values.shape[longest]
        spots.append(tuple(where))
    return values.at[spots[0]].set(least).at[spots[1]].set(top_value)


def level_of(key, extent, cuts, smallest, top_value):
    def one(position, parts):
        steps = jax.random.uniform(jax.random.fold_in(jax.random.fold_in(key, 6), position), (parts,), jnp.float32, smallest / len(cuts), top_value / len(cuts))
        return jnp.repeat(jnp.exp(steps), extent[position] // parts).reshape((-1,) + (1,) * (len(extent) - position - 1))

    level = one(*cuts[0])
    for cut in cuts[1:]:
        level = level * one(*cut)
    return level


def centred(own_key, extent, width, most, shards=(), kind=jnp.bfloat16):
    values = jax.random.normal(own_key, extent, jnp.float32) * width
    if len(shards) > 0:
        values = level_of(own_key, extent, shards, -0.22, 0.18) * values
    return jnp.clip(values, min=-most, max=most).astype(kind)


def setup_inputs(seed: int = 0) -> dict:
    seeds = jax.random.split(jax.random.key(seed), 8)
    return {
        "velocity": draw_velocity(jax.random.fold_in(seeds[7], 71), 0),
        "fields_prev": draw_fields_prev(jax.random.fold_in(seeds[7], 71), 0),
        "fields_now": draw_fields_now(jax.random.fold_in(seeds[7], 71), 0),
        "source_cells": place_ends(jax.random.randint(seeds[3], (SHOTS, SRC_TOTAL), 4 * NX * NY, (PLANES - 4) * NX * NY), jax.random.fold_in(seeds[3], 1), 4 * NX * NY, ((PLANES - 4) * NX * NY) - 1).astype(jnp.int32),
        "source_traces": centred(seeds[4], (SHOTS, STEPS, SRC_TOTAL), 1.0, 6.0, ((0, 16), (2, 16)), jnp.float32),
        "receiver_cells": place_ends(jax.random.randint(seeds[5], (SHOTS, RECV_TOTAL), 4 * NX * NY, (PLANES - 4) * NX * NY), jax.random.fold_in(seeds[5], 1), 4 * NX * NY, ((PLANES - 4) * NX * NY) - 1).astype(jnp.int32),
        "receiver_traces": centred(seeds[6], (SHOTS, STEPS, RECV_TOTAL), 1.0, 6.0, ((0, 16), (2, 16)), jnp.float32),
    }


STENCIL = (-205.0 / 72.0, 8.0 / 5.0, -1.0 / 5.0, 8.0 / 315.0, -1.0 / 560.0)


def laplacian(field):
    depth_rows = field.shape[-3]
    width_x = field.shape[-2]
    width_y = field.shape[-1]
    centre = field[..., 4:depth_rows - 4, :, :]
    padded = jnp.pad(centre, [(0, 0)] * (centre.ndim - 2) + [(4, 4), (4, 4)])
    result = (3.0 * STENCIL[0]) * centre
    for reach in range(1, 5):
        result = result + STENCIL[reach] * (field[..., 4 + reach:depth_rows - 4 + reach, :, :] + field[..., 4 - reach:depth_rows - 4 - reach, :, :])
        result = result + STENCIL[reach] * (padded[..., 4 + reach:4 + reach + width_x, 4:4 + width_y] + padded[..., 4 - reach:4 - reach + width_x, 4:4 + width_y])
        result = result + STENCIL[reach] * (padded[..., 4:4 + width_x, 4 + reach:4 + reach + width_y] + padded[..., 4:4 + width_x, 4 - reach:4 - reach + width_y])
    return result


def inject(field, source_index, source_amps, receiver_index, receiver_amps):
    flattened = field.reshape(2, -1)
    source_row = flattened[0].at[source_index].add(source_amps)
    adjoint_row = flattened[1].at[receiver_index].add(receiver_amps)
    return jnp.stack((source_row, adjoint_row)).reshape(field.shape)


def reference(velocity, fields_prev, fields_now, source_cells, source_traces, receiver_cells, receiver_traces):
    slab_cells = PLANES * NX * NY
    source_offset = (jnp.arange(SRC_TOTAL, dtype=jnp.int32) // SRC_DEV) * slab_cells
    receiver_offset = (jnp.arange(RECV_TOTAL, dtype=jnp.int32) // RECV_DEV) * slab_cells
    courant_sq = velocity * velocity

    def one_shot(summed, inputs):
        previous, current, src_cells, src_amps, rec_cells, rec_amps = inputs
        imaging = jnp.zeros_like(velocity)
        for step_index in range(STEPS):
            padded = jnp.pad(current, ((0, 0), (4, 4), (0, 0), (0, 0)))
            advanced = 2.0 * current - previous + courant_sq * laplacian(padded)
            advanced = inject(advanced, (src_cells + source_offset).astype(jnp.int32), src_amps[step_index],
                              (rec_cells + receiver_offset).astype(jnp.int32), rec_amps[step_index])
            imaging = imaging + (advanced[0] - 2.0 * current[0] + previous[0]) * current[1]
            previous, current = current, advanced
        return summed + imaging, (previous, current)

    summed, outputs = lax.scan(one_shot, jnp.zeros_like(velocity),
                               (fields_prev, fields_now, source_cells, source_traces, receiver_cells, receiver_traces))
    factor = -2.0 / (SHOTS * STEPS)
    gradient = factor * summed / (velocity * velocity * velocity)
    return gradient, outputs[0], outputs[1]
```

```python
import functools

import jax
import jax.numpy as jnp
from jax import lax
from jax.experimental import pallas as pl
from jax.experimental.pallas import tpu as pltpu
from jax.sharding import PartitionSpec as P

STEPS = 8
PLANES = 16
NX = 64
NY = 128
SCALE = 5040.0
TAPS = (8064.0, -1008.0, 128.0, -9.0)
CENTRE = 3.0 * -14350.0
F32 = jnp.float32
BF16 = jnp.bfloat16
VMEM_LIMIT = 24 * 1024 * 1024


def y_matrix():
    row = lax.broadcasted_iota(jnp.int32, (2 * NY, NY), 0)
    col = lax.broadcasted_iota(jnp.int32, (2 * NY, NY), 1)
    apart = jnp.abs((row & (NY - 1)) - col)
    out = jnp.zeros((2 * NY, NY), F32)
    for reach, tap in enumerate(TAPS, 1):
        out = jnp.where(apart == reach, tap, out)
    return out.astype(BF16)


def lateral(src, first, count, mat_ref, dest):
    for field in range(2):
        rows = src[field, pl.ds(first, count)].reshape(count * NX, NY)
        high = rows.astype(BF16)
        low = (rows - high.astype(F32)).astype(BF16)
        both = jnp.concatenate([high, low], axis=1)
        dest[field, pl.ds(0, count)] = jnp.dot(
            both, mat_ref[...], preferred_element_type=F32
        ).reshape(count, 8, 8, NY)


def advance(src, first, prev, prev_first, dest, dest_first, vel, vel_first, count, mat_ref, part,
            image=None, image_first=0, inj=None, inj_first=0, unroll=2):
    lateral(src, first, count, mat_ref, part)
    sub = lax.broadcasted_iota(jnp.int32, (8, NY), 0)
    top, bottom = sub == 0, sub == 7

    def plane(p, carry):
        tiles = []
        for field in range(2):
            own = [src[field, first + p, j] for j in range(8)]
            left = [jnp.where(top, 0.0, pltpu.roll(own[j], 1, 0)) for j in range(4, 8)]
            right = [jnp.where(bottom, 0.0, pltpu.roll(own[j], 7, 0)) for j in range(4)]
            tiles.append(left + own + right)
        for j in range(8):
            speed = vel[vel_first + p, j]
            for field in range(2):
                line = tiles[field]
                here = line[j + 4]
                total = CENTRE * here + part[field, p, j]
                for reach, tap in enumerate(TAPS, 1):
                    pair = (line[j + 4 + reach] + line[j + 4 - reach]) + (
                        src[field, first + p + reach, j] + src[field, first + p - reach, j]
                    )
                    total = total + tap * pair
                change = speed * total
                if field == 1 and inj is not None:
                    change = change + inj[inj_first + p, j]
                dest[field, dest_first + p, j] = (here + here) - prev[field, prev_first + p, j] + change
                if field == 0 and image is not None:
                    image[image_first + p, j] += change * tiles[1][j + 4]
        return carry

    lax.fori_loop(0, count, plane, 0, unroll=unroll)


def add_sources(cells, amps, step, dest, dest_first, image, factor, factor_first):
    sub = lax.broadcasted_iota(jnp.int32, (8, NY), 0)
    lane = lax.broadcasted_iota(jnp.int32, (8, NY), 1)
    for n in range(cells.shape[1]):
        cell = cells[0, n]
        z, x, y = cell >> 13, (cell >> 7) & (NX - 1), cell & (NY - 1)
        j, s = x & 7, x >> 3
        amount = jnp.where((sub == s) & (lane == y), amps[0, step, n], 0.0)
        dest[0, dest_first + z, j] += amount
        image[z, j] += amount * factor[1, factor_first + z, j]


def two_steps(step, now, prev, vel, mid, last, last_first, image, inj, cells, amps, mat_ref, part):
    run = functools.partial(advance, mat_ref=mat_ref, part=part)
    for chunk in range(6):
        lo = 4 * chunk
        run(now, lo + 4, prev, lo, mid, lo, vel, lo, 4,
            image=image if 1 <= chunk <= 4 else None, image_first=lo - 4,
            inj=inj.at[0] if 2 <= chunk <= 3 else None, inj_first=lo - 8)
    add_sources(cells, amps, step, mid, 4, image, now, 8)
    for chunk in range(4):
        lo = 4 * chunk
        run(mid, lo + 4, now, lo + 8, last, last_first + lo, vel, lo + 4, 4,
            image=image, image_first=lo,
            inj=inj.at[1] if 1 <= chunk <= 2 else None, inj_first=lo - 4)
    add_sources(cells, amps, step + 1, last, last_first, image, mid, 4)


def to_tiles(src, base, dest_tile):
    for j in range(8):
        dest_tile(j, src[pl.ds(base + j, 8, stride=8), :])


def inject_kernel(cells, amps, out):
    count = cells.shape[1]
    cell = cells[...]
    z, x, y = cell >> 13, (cell >> 7) & (NX - 1), cell & (NY - 1)
    row = (z - 4) * NX + (x & 7) * 8 + (x >> 3)
    hit = (lax.broadcasted_iota(jnp.int32, (8 * NX, count), 0) == row).astype(F32).astype(BF16)
    hits = jnp.concatenate([hit, hit, hit], axis=1)
    lane = lax.broadcasted_iota(jnp.int32, (NY, count), 0) == y
    for pair in range(STEPS // 2):
        sides = []
        for step in (2 * pair, 2 * pair + 1):
            amount = amps[0, pl.ds(step, 1), :]
            high = amount.astype(BF16).astype(F32)
            rest = amount - high
            middle = rest.astype(BF16).astype(F32)
            low = rest - middle
            sides.append(jnp.concatenate(
                [jnp.where(lane, part, 0.0).astype(BF16) for part in (high, middle, low)], axis=1))
        both = jnp.concatenate(sides, axis=0)
        dense = lax.dot_general(hits, both, (((1,), (1,)), ((), ())), preferred_element_type=F32)
        for side in range(2):
            out[2 * pair + side] = dense[:, side * NY:(side + 1) * NY].reshape(8, 8, 8, NY)


def first_kernel(cells, amps, gathered, low_msg, high_msg, prev_in, now_in, inj,
                 low_out, high_out, mid, vel, image, mat_ref, part, now, prev, last):
    mat_ref[...] = y_matrix()
    image[...] = jnp.zeros_like(image)

    def vel_plane(p, carry):
        for j in range(8):
            line = gathered[pl.ds((j // 4) * 96 + p * 4 + j % 4, 8, stride=192), :]
            vel[p, j] = line * line * (1.0 / SCALE)
        return carry

    lax.fori_loop(0, 24, vel_plane, 0, unroll=2)

    def convert(src, count, src_first, per_field, dest, dest_first):
        def plane(p, carry):
            for field in range(2):
                base = (field * per_field + src_first + p) * NX
                for j in range(8):
                    dest[field, dest_first + p, j] = src[pl.ds(base + j, 8, stride=8), :]
            return carry

        lax.fori_loop(0, count, plane, 0, unroll=2)

    convert(low_msg, 8, 0, 12, now, 0)
    convert(now_in, 16, 0, 16, now, 8)
    convert(high_msg, 8, 0, 12, now, 24)
    convert(low_msg, 4, 8, 12, prev, 0)
    convert(prev_in, 16, 0, 16, prev, 4)
    convert(high_msg, 4, 8, 12, prev, 20)
    two_steps(0, now, prev, vel, mid, last, 0, image, inj, cells, amps, mat_ref, part)
    low_out[...] = last[:, 0:8]
    high_out[...] = last[:, 8:16]


def gather_now(below, low, high, above, now):
    def plane(p, carry):
        for field in range(2):
            for n, src in enumerate((below, low, high, above)):
                now[field, 8 * n + p] = src[field, p]
        return carry

    lax.fori_loop(0, 8, plane, 0, unroll=2)


def middle_kernel(step, cells, amps, below, low, high, above, prev, vel, image_in, inj,
                  low_out, high_out, mid, image, mat_ref, part, now, last):
    mat_ref[...] = y_matrix()
    image[...] = image_in[...]
    gather_now(below, low, high, above, now)
    two_steps(step, now, prev, vel, mid, last, 0, image, inj, cells, amps, mat_ref, part)
    low_out[...] = last[:, 0:8]
    high_out[...] = last[:, 8:16]


def last_kernel(step, cells, amps, below, low, high, above, prev, vel, image_in, inj,
                before, after, image_out, mat_ref, part, now, mid, last, image):
    mat_ref[...] = y_matrix()
    image[...] = image_in[...]
    gather_now(below, low, high, above, now)
    two_steps(step, now, prev, vel, mid, last, 0, image, inj, cells, amps, mat_ref, part)

    def plane(p, carry):
        for j in range(8):
            image_out[pl.ds((j // 4) * 64 + p * 4 + j % 4, 8, stride=128), :] = image[p, j]
            for field in range(2):
                base = (field * 16 + p) * NX + j
                before[pl.ds(base, 8, stride=8), :] = mid[field, 4 + p, j]
                after[pl.ds(base, 8, stride=8), :] = last[field, p, j]
        return carry

    lax.fori_loop(0, PLANES, plane, 0, unroll=2)


def tiles(*lead):
    return jax.ShapeDtypeStruct((*lead, 8, 8, NY), F32)


def call(kernel, smem, args, outs, scratch, flops):
    whole = pl.BlockSpec(memory_space=pltpu.VMEM)
    return pl.pallas_call(
        kernel,
        in_specs=[pl.BlockSpec(memory_space=pltpu.SMEM)] * smem + [whole] * (len(args) - smem),
        out_specs=jax.tree.map(lambda _: whole, outs),
        out_shape=outs,
        scratch_shapes=scratch,
        compiler_params=pltpu.CompilerParams(vmem_limit_bytes=VMEM_LIMIT),
        cost_estimate=pl.CostEstimate(flops=flops, bytes_accessed=4 << 20, transcendentals=0),
    )(*args)


def body(
    velocity, fields_prev, fields_now, source_cells, source_traces, receiver_cells, receiver_traces
):
    slabs, shots = lax.axis_size("slab"), lax.axis_size("shot")
    up = [(i, i + 1) for i in range(slabs - 1)]
    down = [(j, i) for i, j in up]

    vel_below = lax.ppermute(velocity[12:], "slab", up)
    vel_above = lax.ppermute(velocity[:4], "slab", down)
    now, prev = fields_now[0], fields_prev[0]
    low_msg = lax.ppermute(jnp.concatenate([now[:, 8:], prev[:, 12:]], axis=1), "slab", up)
    high_msg = lax.ppermute(jnp.concatenate([now[:, :8], prev[:, :4]], axis=1), "slab", down)
    own = jnp.concatenate([vel_below, velocity, vel_above], axis=0).reshape(1, 96, NY)
    gathered = lax.all_to_all(jnp.broadcast_to(own, (shots, 96, NY)), "shot", 0, 0, tiled=True)

    whole = pl.BlockSpec(memory_space=pltpu.VMEM)
    inj = pl.pallas_call(
        inject_kernel,
        in_specs=[whole, whole],
        out_specs=whole,
        out_shape=tiles(STEPS, 8),
        compiler_params=pltpu.CompilerParams(vmem_limit_bytes=VMEM_LIMIT),
        cost_estimate=pl.CostEstimate(flops=1 << 30, bytes_accessed=2 << 20, transcendentals=0),
    )(receiver_cells, receiver_traces)

    half, ext = tiles(2, 8), tiles(2, 24)
    vm = lambda s: pltpu.VMEM(s.shape, s.dtype)
    common = [pltpu.VMEM((2 * NY, NY), BF16), vm(tiles(2, 4)), vm(tiles(2, 32))]
    flops = 1 << 27
    low, high, mid, vel, image = call(
        first_kernel, 2,
        (source_cells, source_traces, gathered.reshape(shots * 96, NY), low_msg.reshape(-1, NY),
         high_msg.reshape(-1, NY), prev.reshape(-1, NY), now.reshape(-1, NY), inj[0:2]),
        (half, half, ext, tiles(24), tiles(16)),
        [*common, vm(ext), vm(tiles(2, 16))], flops)
    for step in range(2, STEPS, 2):
        below = lax.ppermute(high, "slab", up)
        above = lax.ppermute(low, "slab", down)
        args = (source_cells, source_traces, below, low, high, above, mid, vel, image, inj[step:step + 2])
        if step < STEPS - 2:
            low, high, mid, image = call(
                functools.partial(middle_kernel, step), 2, args, (half, half, ext, tiles(16)),
                [*common, vm(tiles(2, 16))], flops)
        else:
            rows = jax.ShapeDtypeStruct((2 * PLANES * NX, NY), F32)
            before, after, terms = call(
                functools.partial(last_kernel, step), 2, args,
                (rows, rows, jax.ShapeDtypeStruct((16 * 64, NY), F32)),
                [*common, vm(ext), vm(tiles(2, 16)), vm(tiles(16))], flops)
    terms = lax.all_to_all(terms.reshape(shots, 64, NY), "shot", 0, 0, tiled=True)
    summed = jnp.sum(terms, axis=0).reshape(velocity.shape)
    gradient = (-2.0 / (shots * STEPS)) * summed / (velocity * velocity * velocity)
    shape = fields_now.shape
    return gradient, before.reshape(shape), after.reshape(shape)


def solution(mesh):
    return jax.shard_map(
        body,
        mesh=mesh,
        in_specs=(
            P("slab", "shot", None),
            P("shot", None, "slab", None, None),
            P("shot", None, "slab", None, None),
            P("shot", "slab"),
            P("shot", None, "slab"),
            P("shot", "slab"),
            P("shot", None, "slab"),
        ),
        out_specs=(
            P("slab", "shot", None),
            P("shot", None, "slab", None, None),
            P("shot", None, "slab", None, None),
        ),
        check_vma=False,
    )
```

```python
import functools

import jax
import jax.numpy as jnp
from jax import lax
from jax.experimental import pallas as pl
from jax.experimental.pallas import tpu as pltpu
from jax.sharding import PartitionSpec as P

STEPS = 8
PLANES = 16
NX = 64
NY = 128
SCALE = 5040.0
TAPS = (8064.0, -1008.0, 128.0, -9.0)
CENTRE = 3.0 * -14350.0
F32 = jnp.float32
BF16 = jnp.bfloat16
VMEM_LIMIT = 20 * 1024 * 1024


def fill_matrix(mat_ref):
    row = lax.broadcasted_iota(jnp.int32, (2 * NY, NY), 0)
    col = lax.broadcasted_iota(jnp.int32, (2 * NY, NY), 1)
    apart = jnp.abs((row & (NY - 1)) - col)
    out = jnp.zeros((2 * NY, NY), F32)
    for reach, tap in enumerate(TAPS, 1):
        out = jnp.where(apart == reach, tap, out)
    mat_ref[...] = out.astype(BF16)


class Rows:
    def __init__(self, *parts):
        self.parts = parts

    def find(self, plane):
        for ref, first, count in self.parts:
            if first <= plane < first + count:
                return ref, plane - first
        raise ValueError(plane)

    def tile(self, field, plane, j):
        ref, at = self.find(plane)
        return ref[field, at, j]

    def chunk(self, field, plane, count):
        ref, at = self.find(plane)
        return ref[field, pl.ds(at, count)]

    def put(self, field, plane, j, value):
        ref, at = self.find(plane)
        ref[field, at, j] = value


def advance(src, prev, dest, vel, first, mat_ref, part, image, inj):
    for field in range(2):
        rows = src.chunk(field, first, 4).reshape(4 * NX, NY)
        high = rows.astype(BF16)
        low = (rows - high.astype(F32)).astype(BF16)
        both = jnp.concatenate([high, low], axis=1)
        part[field] = jnp.dot(both, mat_ref[...], preferred_element_type=F32).reshape(4, 8, 8, NY)
    sub = lax.broadcasted_iota(jnp.int32, (8, NY), 0)
    top, bottom = sub == 0, sub == 7
    for p in range(4):
        plane = first + p
        imaged = 0 <= plane < PLANES
        tiles = []
        for field in range(2):
            own = [src.tile(field, plane, j) for j in range(8)]
            left = [jnp.where(top, 0.0, pltpu.roll(own[j], 1, 0)) for j in range(4, 8)]
            right = [jnp.where(bottom, 0.0, pltpu.roll(own[j], 7, 0)) for j in range(4)]
            tiles.append(left + own + right)
        for j in range(8):
            speed = vel[plane + 4, j]
            for field in range(2):
                line = tiles[field]
                here = line[j + 4]
                total = CENTRE * here + part[field, p, j]
                for reach, tap in enumerate(TAPS, 1):
                    pair = (line[j + 4 + reach] + line[j + 4 - reach]) + (
                        src.tile(field, plane + reach, j) + src.tile(field, plane - reach, j)
                    )
                    total = total + tap * pair
                change = speed * total
                if field == 1 and 4 <= plane < 12:
                    change = change + inj[plane - 4, j]
                dest.put(field, plane, j, (here + here) - prev.tile(field, plane, j) + change)
                if field == 0 and imaged:
                    image[plane, j] += change * tiles[1][j + 4]


def add_sources(cells, amps, step, dest, dest_plane, image, factors, planes):
    sub = lax.broadcasted_iota(jnp.int32, (8, NY), 0)
    lane = lax.broadcasted_iota(jnp.int32, (8, NY), 1)
    for n in range(cells.shape[1]):
        cell = cells[0, n]
        z, x, y = cell >> 13, (cell >> 7) & (NX - 1), cell & (NY - 1)
        j, s = x & 7, x >> 3
        for ref, ref_plane, lo, hi in factors:
            lo, hi = max(lo, planes[0]), min(hi, planes[1])

            @pl.when((z >= lo) & (z <= hi))
            def _():
                zc = jnp.clip(z, lo, hi)
                amount = jnp.where((sub == s) & (lane == y), amps[0, step, n], 0.0)
                dest[0, zc - dest_plane, j] += amount
                image[zc, j] += amount * ref[1, zc - ref_plane, j]


def half_block(side, first_half, step, now_parts, prev_parts, mids, outs, vel, image, inj, cells, amps, mat_ref, part):
    now, prev = Rows(*now_parts), Rows(*prev_parts)
    mid = Rows(*mids)
    run = functools.partial(advance, vel=vel, mat_ref=mat_ref, image=image)
    if side == 0:
        chunks = (-4, 0, 4, 8) if first_half else (-4, 0)
    else:
        chunks = (4, 8, 12, 16) if first_half else (12, 16)
    for n, lo in enumerate(chunks):
        run(now, prev, mid, first=lo, part=part.at[n % 2], inj=inj.at[0])
    own_mid, own_first, _ = mids[side] if len(mids) == 2 else mids[0]
    if first_half:
        factors = [(ref, first, first, first + count - 1) for ref, first, count in now_parts if 0 <= first < 16]
        add_sources(cells, amps, step, own_mid, own_first, image, factors, (4, 11))
    base = 8 * side
    out = Rows((outs, base, 8))
    for n, lo in enumerate((base, base + 4)):
        run(mid, now, out, first=lo, part=part.at[n % 2], inj=inj.at[1])
    factors = [(ref, first, first, first + count - 1) for ref, first, count in mids]
    planes = (4, 7) if side == 0 else (8, 11)
    factors = [f for f in factors if max(f[2], planes[0]) <= min(f[3], planes[1])]
    add_sources(cells, amps, step + 1, outs, base, image, factors, planes)


def first_half_kernel(side, step, zero_end, cells, amps, beyond, low, high, prev_lo, prev_hi, vel, image_in, inj, mat_ref,
                      out, mid, image, beyond_out, part, *, prev_split):
    del beyond, image_in

    @pl.when(zero_end[0] == 1)
    def _():
        beyond_out[...] = jnp.zeros_like(beyond_out)

    if side == 0:
        now = ((beyond_out, -8, 8), (low, 0, 8), (high, 8, 8))
        mids = ((mid, -4, 16),)
    else:
        now = ((low, 0, 8), (high, 8, 8), (beyond_out, 16, 8))
        mids = ((mid, 4, 16),)
    prev = ((prev_lo, -4, prev_split), (prev_hi, prev_split - 4, 24 - prev_split))
    half_block(side, True, step, now, prev, mids, out, vel, image, inj, cells, amps, mat_ref, part)


def second_half_kernel(side, step, zero_end, cells, amps, beyond, low, high, prev_lo, prev_hi, other_mid, vel, image_in, inj,
                       mat_ref, out, mid, image, beyond_out, part, *, prev_split):
    del beyond, image_in

    @pl.when(zero_end[0] == 1)
    def _():
        beyond_out[...] = jnp.zeros_like(beyond_out)

    if side == 0:
        now = ((beyond_out, -8, 8), (low, 0, 8), (high, 8, 8))
        mids = ((mid, -4, 8), (other_mid, 4, 16))
    else:
        now = ((low, 0, 8), (high, 8, 8), (beyond_out, 16, 8))
        mids = ((other_mid, -4, 16), (mid, 12, 8))
    prev = ((prev_lo, -4, prev_split), (prev_hi, prev_split - 4, 24 - prev_split))
    half_block(side, False, step, now, prev, mids, out, vel, image, inj, cells, amps, mat_ref, part)


def pack_kernel(prev_in, now_in, up_msg, down_msg, low, high, prev, mat_ref):
    fill_matrix(mat_ref)

    def plane(src, field, p, *dests):
        for j in range(8):
            tile = src[pl.ds((field * PLANES + p) * NX + j, 8, stride=8), :]
            for ref, at in dests:
                ref[field, at, j] = tile

    for field in range(2):
        for p in range(8):
            plane(now_in, field, p, (low, p), (down_msg, p))
        for p in range(8):
            plane(now_in, field, 8 + p, (high, p), (up_msg, p))
        for p in range(PLANES):
            more = ((down_msg, 8 + p),) if p < 4 else ((up_msg, p - 4),) if p >= 12 else ()
            plane(prev_in, field, p, (prev, p), *more)


def spread_kernel(below, own, above, out):
    rows = jnp.concatenate([below[...], own[...], above[...]], axis=0)
    for shot in range(16):
        out[pl.ds(shot * 96, 96), :] = rows


def inject_kernel(cells, amps, out):
    count = cells.shape[1]
    cell = cells[...]
    z, x, y = cell >> 13, (cell >> 7) & (NX - 1), cell & (NY - 1)
    row = (z - 4) * NX + (x & 7) * 8 + (x >> 3)
    hit = (lax.broadcasted_iota(jnp.int32, (8 * NX, count), 0) == row).astype(F32).astype(BF16)
    hits = jnp.concatenate([hit, hit, hit], axis=1)
    lane = lax.broadcasted_iota(jnp.int32, (NY, count), 0) == y
    for pair in range(STEPS // 2):
        sides = []
        for step in (2 * pair, 2 * pair + 1):
            amount = amps[0, pl.ds(step, 1), :]
            high = amount.astype(BF16).astype(F32)
            rest = amount - high
            middle = rest.astype(BF16).astype(F32)
            low = rest - middle
            sides.append(jnp.concatenate(
                [jnp.where(lane, part, 0.0).astype(BF16) for part in (high, middle, low)], axis=1))
        both = jnp.concatenate(sides, axis=0)
        dense = lax.dot_general(hits, both, (((1,), (1,)), ((), ())), preferred_element_type=F32)
        for side in range(2):
            out[2 * pair + side] = dense[:, side * NY:(side + 1) * NY].reshape(8, 8, 8, NY)


def open_kernel(ends, gathered, below_msg, above_msg, prev, vel, image, below, above, prev_lo, prev_hi):
    image[...] = jnp.zeros_like(image)
    at_start, at_end = ends[0] == 1, ends[1] == 1

    for p in range(24):
        for j in range(8):
            line = gathered[pl.ds((j // 4) * 96 + p * 4 + j % 4, 8, stride=192), :]
            vel[p, j] = line * line * (1.0 / SCALE)
    below[...] = below_msg[:, :8]
    above[...] = above_msg[:, :8]
    prev_lo[:, 0:4] = below_msg[:, 8:]
    prev_lo[:, 4:12] = prev[:, :8]
    prev_hi[:, 0:8] = prev[:, 8:]
    prev_hi[:, 8:12] = above_msg[:, 8:]

    @pl.when(at_start)
    def _():
        vel[0:4] = jnp.zeros((4, 8, 8, NY), F32)
        prev_lo[:, 0:4] = jnp.zeros((2, 4, 8, 8, NY), F32)

    @pl.when(at_end)
    def _():
        vel[20:24] = jnp.zeros((4, 8, 8, NY), F32)
        prev_hi[:, 8:12] = jnp.zeros((2, 4, 8, 8, NY), F32)


def terms_kernel(image, out):
    for p in range(PLANES):
        for j in range(8):
            out[pl.ds((j // 4) * 64 + p * 4 + j % 4, 8, stride=128), :] = image[p, j]


def close_kernel(mid_lo, mid_hi, low, high, before, after, *, split):
    mid = Rows((mid_lo, -4, split), (mid_hi, split - 4, 24 - split))
    last = Rows((low, 0, 8), (high, 8, 8))
    for field in range(2):
        for p in range(PLANES):
            for j in range(8):
                rows = pl.ds((field * PLANES + p) * NX + j, 8, stride=8)
                before[rows, :] = mid.tile(field, p, j)
                after[rows, :] = last.tile(field, p, j)


def tiles(*lead):
    return jax.ShapeDtypeStruct((*lead, 8, 8, NY), F32)


def rows_of(count):
    return jax.ShapeDtypeStruct((count, NY), F32)


def call(kernel, args, outs, flops, smem=0, scratch=(), aliases=None):
    whole = pl.BlockSpec(memory_space=pltpu.VMEM)
    return pl.pallas_call(
        kernel,
        in_specs=[pl.BlockSpec(memory_space=pltpu.SMEM)] * smem + [whole] * (len(args) - smem),
        out_specs=jax.tree.map(lambda _: whole, outs),
        out_shape=outs,
        scratch_shapes=list(scratch),
        input_output_aliases=aliases or {},
        compiler_params=pltpu.CompilerParams(vmem_limit_bytes=VMEM_LIMIT),
        cost_estimate=pl.CostEstimate(flops=flops, bytes_accessed=1 << 20, transcendentals=0),
    )(*args)


def body(
    velocity, fields_prev, fields_now, source_cells, source_traces, receiver_cells, receiver_traces
):
    slabs, shots = lax.axis_size("slab"), lax.axis_size("shot")
    up = [(i, (i + 1) % slabs) for i in range(slabs)]
    down = [(j, i) for i, j in up]
    slab = lax.axis_index("slab")
    at_start = (slab == 0).astype(jnp.int32).reshape(1)
    at_end = (slab == slabs - 1).astype(jnp.int32).reshape(1)

    vel_rows = velocity.reshape(PLANES * 4, NY)
    vel_below = lax.ppermute(vel_rows[48:], "slab", up)
    vel_above = lax.ppermute(vel_rows[:16], "slab", down)
    half, ext = tiles(2, 8), tiles(2, 24)
    mat = jax.ShapeDtypeStruct((2 * NY, NY), BF16)
    up_msg, down_msg, low, high, prev, mat = call(
        pack_kernel, (fields_prev.reshape(-1, NY), fields_now.reshape(-1, NY)),
        (tiles(2, 12), tiles(2, 12), half, half, tiles(2, 16), mat), 1 << 22)
    below_msg = lax.ppermute(up_msg, "slab", up)
    above_msg = lax.ppermute(down_msg, "slab", down)
    spread = call(spread_kernel, (vel_below, vel_rows, vel_above), rows_of(shots * 96), 1 << 20)
    gathered = lax.all_to_all(spread.reshape(shots, 96, NY), "shot", 0, 0, tiled=True)
    inj = call(inject_kernel, (receiver_cells, receiver_traces), tiles(STEPS, 8), 1 << 27)
    vel, image, below, above, prev_lo, prev_hi = call(
        open_kernel, (jnp.concatenate([at_start, at_end]), gathered.reshape(shots * 96, NY), below_msg, above_msg, prev),
        (tiles(24), tiles(16), half, half, tiles(2, 12), tiles(2, 12)), 1 << 22, smem=1)

    split = 12
    part = [pltpu.VMEM((2, 2, 4, 8, 8, NY), F32)]
    for step in range(0, STEPS, 2):
        order = (1, 0) if step % 4 == 0 else (0, 1)
        news, mids = {}, {}
        for n, side in enumerate(order):
            beyond, flag = (below, at_start) if side == 0 else (above, at_end)
            args = [flag, source_cells, source_traces, beyond, low, high, prev_lo, prev_hi]
            if n == 1:
                args.append(mids[order[0]])
            at = len(args)
            args += [vel, image, inj[step:step + 2], mat]
            kernel = first_half_kernel if n == 0 else second_half_kernel
            news[side], mids[side], image, _ = call(
                functools.partial(kernel, side, step, prev_split=split), args,
                (half, tiles(2, 16 if n == 0 else 8), tiles(16), half), 1 << 26,
                smem=3, scratch=part, aliases={3: 3, at + 1: 2})
            if step < STEPS - 2:
                if side == 1:
                    next_below = lax.ppermute(news[1], "slab", up)
                else:
                    next_above = lax.ppermute(news[0], "slab", down)
        low, high = news[0], news[1]
        prev_lo, prev_hi = mids[0], mids[1]
        split = 16 if order[0] == 0 else 8
        below, above = next_below, next_above

    terms = call(terms_kernel, (image,), rows_of(shots * 64), 1 << 20)
    terms = lax.all_to_all(terms.reshape(shots, 64, NY), "shot", 0, 0, tiled=True)
    before, after = call(
        functools.partial(close_kernel, split=split), (prev_lo, prev_hi, low, high),
        (rows_of(2 * PLANES * NX), rows_of(2 * PLANES * NX)), 1 << 22)
    summed = jnp.sum(terms, axis=0).reshape(velocity.shape)
    gradient = (-2.0 / (shots * STEPS)) * summed / (velocity * velocity * velocity)
    shape = fields_now.shape
    return gradient, before.reshape(shape), after.reshape(shape)


def solution(mesh):
    return jax.shard_map(
        body,
        mesh=mesh,
        in_specs=(
            P("slab", "shot", None),
            P("shot", None, "slab", None, None),
            P("shot", None, "slab", None, None),
            P("shot", "slab"),
            P("shot", None, "slab"),
            P("shot", "slab"),
            P("shot", None, "slab"),
        ),
        out_specs=(
            P("slab", "shot", None),
            P("shot", None, "slab", None, None),
            P("shot", None, "slab", None, None),
        ),
        check_vma=False,
    )
```

```python
import functools

import jax
import jax.numpy as jnp
from jax import lax
from jax.experimental import pallas as pl
from jax.experimental.pallas import tpu as pltpu
from jax.sharding import PartitionSpec as P

STEPS = 8
PLANES = 16
NX = 64
NY = 128
SCALE = 5040.0
TAPS = (8064.0, -1008.0, 128.0, -9.0)
CENTRE = 3.0 * -14350.0
F32 = jnp.float32
BF16 = jnp.bfloat16
VMEM_LIMIT = 16 * 1024 * 1024


def fill_matrix(mat_ref):
    row = lax.broadcasted_iota(jnp.int32, (2 * NY, NY), 0)
    col = lax.broadcasted_iota(jnp.int32, (2 * NY, NY), 1)
    apart = jnp.abs((row & (NY - 1)) - col)
    out = jnp.zeros((2 * NY, NY), F32)
    for reach, tap in enumerate(TAPS, 1):
        out = jnp.where(apart == reach, tap, out)
    mat_ref[...] = out.astype(BF16)


class Rows:
    def __init__(self, *parts):
        self.parts = parts

    def find(self, plane):
        for ref, first, count in self.parts:
            if first <= plane < first + count:
                return ref, plane - first
        raise ValueError(plane)

    def tile(self, plane, j):
        ref, at = self.find(plane)
        return ref[at, j]

    def chunk(self, plane, count):
        ref, at = self.find(plane)
        return ref[pl.ds(at, count)]

    def put(self, plane, j, value):
        ref, at = self.find(plane)
        ref[at, j] = value


def advance(src, prev, dest, vel, first, mat_ref, part, inj, see):
    rows = src.chunk(first, 4).reshape(4 * NX, NY)
    high = rows.astype(BF16)
    low = (rows - high.astype(F32)).astype(BF16)
    both = jnp.concatenate([high, low], axis=1)
    part[...] = jnp.dot(both, mat_ref[...], preferred_element_type=F32).reshape(4, 8, 8, NY)
    sub = lax.broadcasted_iota(jnp.int32, (8, NY), 0)
    top, bottom = sub == 0, sub == 7
    for p in range(4):
        plane = first + p
        own = [src.tile(plane, j) for j in range(8)]
        left = [jnp.where(top, 0.0, pltpu.roll(own[j], 1, 0)) for j in range(4, 8)]
        right = [jnp.where(bottom, 0.0, pltpu.roll(own[j], 7, 0)) for j in range(4)]
        line = left + own + right
        for j in range(8):
            here = line[j + 4]
            total = CENTRE * here + part[p, j]
            for reach, tap in enumerate(TAPS, 1):
                pair = (line[j + 4 + reach] + line[j + 4 - reach]) + (
                    src.tile(plane + reach, j) + src.tile(plane - reach, j)
                )
                total = total + tap * pair
            change = vel.tile(plane, j) * total
            if 4 <= plane < 12:
                change = change + inj[plane - 4, j]
            dest.put(plane, j, (here + here) - prev.tile(plane, j) + change)
            if 0 <= plane < PLANES:
                see(plane, j, change, here)


class Natural:
    def __init__(self, ref, field):
        self.ref, self.field = ref, field

    def tile(self, plane, j):
        return self.ref[pl.ds((self.field * PLANES + plane) * NX + j, 8, stride=8), :]


def half_kernel(*refs, side, field, now_at, prev_at, vel_at, mid_at, masked, ride, send):
    refs = list(refs)
    take = lambda count: [refs.pop(0) for _ in range(count)]
    rows = lambda some, at: Rows(*[(ref, *where) for ref, where in zip(some, at)])
    keep, mat_ref, inj = take(3)
    vel = rows(take(len(vel_at)), vel_at)
    now_refs = take(len(now_at))
    prev = Natural(take(1)[0], field) if prev_at is None else rows(take(len(prev_at)), prev_at)
    other_mid = take(max(len(mid_at) - 1, 0))
    if field == 1:
        changes, image_in = take(2)
        del image_in
    take(1)
    out, extra = take(2)
    mid = take(1) if mid_at else []
    message = take(1)[0] if send else None
    part, beyond = refs
    if masked:
        beyond = now_refs[0]
    else:
        inside = keep[...] > 0.0
        for p in range(now_at[0][1]):
            for j in range(8):
                beyond[p, j] = jnp.where(inside, now_refs[0][p, j], 0.0)
    now = rows([beyond, *now_refs[1:]], now_at)
    base = 8 * side
    last = Rows((out, base, 8))
    if mid_at:
        mids = rows([*mid, *other_mid], mid_at)
        starts = range(mid_at[0][0], sum(mid_at[0]), 4)
        seen = [p for p in range(mid_at[0][0], sum(mid_at[0])) if 0 <= p < PLANES]

    def see(first):
        def change_out(plane, j, change, here):
            extra[plane - first, j] = change

        def image_out(plane, j, change, here):
            extra[plane, j] += changes[plane - first, j] * here

        return change_out if field == 0 else image_out

    run = functools.partial(advance, vel=vel, mat_ref=mat_ref)
    skip = 0
    if mid_at:
        for n, lo in enumerate(starts):
            run(now, prev, mids, first=lo, part=part.at[n % 2], inj=inj.at[0], see=see(seen[0]))
        now, prev, skip = mids, now, len(seen)
    for n, lo in enumerate((base, base + 4)):
        run(now, prev, last, first=lo, part=part.at[n % 2], inj=inj.at[1 if mid_at else 0], see=see(base - skip))
    border = 12 if side else 0
    for p in range(4):
        for j in range(8):
            if ride:
                out[8 + p, j] = vel.tile(border + p, j)
            if send:
                message[p, j] = out[border - base + p, j]


def edge_kernel(keep, message, out):
    inside = keep[...] > 0.0
    for p in range(4):
        for j in range(8):
            out[p, j] = jnp.where(inside, message[8 + p, j], 0.0)


def pack_kernel(now_in, up_0, down_0, up_1, down_1, low_0, high_0, low_1, high_1, mat_ref):
    fill_matrix(mat_ref)
    for field, (up_msg, down_msg, low, high) in enumerate(((up_0, down_0, low_0, high_0), (up_1, down_1, low_1, high_1))):
        now = Natural(now_in, field)
        for p in range(PLANES):
            for j in range(8):
                tile = now.tile(p, j)
                (high if p >= 8 else low)[p % 8, j] = tile
                if p < 4:
                    down_msg[p, j] = tile
                if p >= 12:
                    up_msg[p - 12, j] = tile


def spread_kernel(own, out):
    for shot in range(16):
        out[pl.ds(shot * 64, 64), :] = own[...]


def dense(cells, amps, step, steps):
    count = cells.shape[1]
    cell = cells[...]
    z, x, y = cell >> 13, (cell >> 7) & (NX - 1), cell & (NY - 1)
    row = (z - 4) * NX + (x & 7) * 8 + (x >> 3)
    hit = (lax.broadcasted_iota(jnp.int32, (8 * NX, count), 0) == row).astype(F32).astype(BF16)
    hits = jnp.concatenate([hit, hit, hit], axis=1)
    lane = lax.broadcasted_iota(jnp.int32, (NY, count), 0) == y
    sides = []
    for at in range(step, step + steps):
        amount = amps[pl.ds(at, 1), :]
        high = amount.astype(BF16).astype(F32)
        rest = amount - high
        middle = rest.astype(BF16).astype(F32)
        low = rest - middle
        sides.append(jnp.concatenate([jnp.where(lane, part, 0.0).astype(BF16) for part in (high, middle, low)], axis=1))
    both = jnp.concatenate(sides, axis=0)
    return lax.dot_general(hits, both, (((1,), (1,)), ((), ())), preferred_element_type=F32)


def inject_kernel(source_cells, source_amps, cells, amps, token, out_0, out_1, *, step, steps):
    del token
    for out, (where, what) in ((out_0, (source_cells, source_amps)), (out_1, (cells, amps))):
        values = dense(where, what, step, steps)
        for side in range(steps):
            out[side] = values[:, side * NY:(side + 1) * NY].reshape(8, 8, 8, NY)


def open_kernel(keep_below, keep_above, gathered, below_0, above_0, below_1, above_1,
                vel, image, below_out_0, above_out_0, below_out_1, above_out_1):
    image[...] = jnp.zeros_like(image)
    for p in range(PLANES):
        for j in range(8):
            line = gathered[pl.ds((j // 4) * 64 + p * 4 + j % 4, 8, stride=128), :]
            vel[p, j] = line * line * (1.0 / SCALE)
    for keep, src, dest in ((keep_below, below_0, below_out_0), (keep_above, above_0, above_out_0),
                            (keep_below, below_1, below_out_1), (keep_above, above_1, above_out_1)):
        inside = keep[...] > 0.0
        for p in range(4):
            for j in range(8):
                dest[p, j] = jnp.where(inside, src[p, j], 0.0)


def terms_kernel(image, velocity, out, factor):
    speed = velocity[...]
    factor[...] = (-2.0 / (16 * STEPS)) / (speed * speed * speed)
    for p in range(PLANES):
        for j in range(8):
            out[pl.ds((j // 4) * 64 + p * 4 + j % 4, 8, stride=128), :] = image[p, j]


def sum_kernel(terms, factor, out):
    total = terms[0:64, :]
    for shot in range(1, 16):
        total = total + terms[pl.ds(64 * shot, 64), :]
    out[...] = total * factor[...]


def close_kernel(before_low_0, before_high_0, low_0, high_0, before_low_1, before_high_1, low_1, high_1, before, after):
    for field, (before_low, before_high, low, high) in enumerate(
            ((before_low_0, before_high_0, low_0, high_0), (before_low_1, before_high_1, low_1, high_1))):
        for p in range(PLANES):
            for j in range(8):
                rows = pl.ds((field * PLANES + p) * NX + j, 8, stride=8)
                before[rows, :] = (before_high if p >= 8 else before_low)[p % 8, j]
                after[rows, :] = (high if p >= 8 else low)[p % 8, j]


def tiles(*lead):
    return jax.ShapeDtypeStruct((*lead, 8, 8, NY), F32)


def rows_of(count):
    return jax.ShapeDtypeStruct((count, NY), F32)


def call(kernel, args, outs, flops, scratch=(), aliases=None):
    whole = pl.BlockSpec(memory_space=pltpu.VMEM)
    return pl.pallas_call(
        kernel,
        in_specs=[whole] * len(args),
        out_specs=jax.tree.map(lambda _: whole, outs),
        out_shape=outs,
        scratch_shapes=list(scratch),
        input_output_aliases=aliases or {},
        compiler_params=pltpu.CompilerParams(vmem_limit_bytes=VMEM_LIMIT),
        cost_estimate=pl.CostEstimate(flops=flops, bytes_accessed=1 << 20, transcendentals=0),
    )(*args)


def body(
    velocity, fields_prev, fields_now, source_cells, source_traces, receiver_cells, receiver_traces
):
    slabs, shots = lax.axis_size("slab"), lax.axis_size("shot")
    up = [(i, (i + 1) % slabs) for i in range(slabs)]
    down = [(j, i) for i, j in up]
    slab = lax.axis_index("slab")
    keep = [jnp.full((8, NY), slab > 0, F32), jnp.full((8, NY), slab < slabs - 1, F32)]

    vel_rows = velocity.reshape(PLANES * 4, NY)
    spread = call(spread_kernel, (vel_rows,), rows_of(shots * 64), 1 << 20)
    gathered = lax.all_to_all(spread.reshape(shots, 64, NY), "shot", 0, 0, tiled=True)
    half, quarter = tiles(8), tiles(4)
    mat = jax.ShapeDtypeStruct((2 * NY, NY), BF16)
    up_0, down_0, up_1, down_1, low_0, high_0, low_1, high_1, mat = call(
        pack_kernel, (fields_now.reshape(-1, NY),), (*[quarter] * 4, *[half] * 4, mat), 1 << 22)
    now = [[low_0, high_0], [low_1, high_1]]
    arrived = [lax.ppermute(a, "slab", way) for a, way in ((up_0, up), (down_0, down), (up_1, up), (down_1, down))]
    few = 128 - source_cells.shape[1]
    marks = (
        jnp.pad(source_cells, ((0, 0), (0, few)), constant_values=4 * NX * NY),
        jnp.pad(source_traces[0], ((0, 0), (0, few))),
        receiver_cells, receiver_traces[0],
    )
    vel, image, *far = call(
        open_kernel, (*keep, gathered.reshape(shots * 64, NY), *arrived), (tiles(16), tiles(16), *[quarter] * 4), 1 << 22)
    beyond = [far[:2], far[2:]]
    vels = [[(vel, (0, 16))], [(vel, (0, 16))]]
    prev_rows = fields_prev.reshape(-1, NY)

    lengths = (1, 2, 2, 2, 1)
    token, step, prev = image, 0, None
    for block, length in enumerate(lengths):
        final = block == len(lengths) - 1
        to_send = 0 if final else 4 * lengths[block + 1]
        order = (1, 0) if block % 2 == 0 else (0, 1)
        news, mids, sent = ([[None, None], [None, None]] for _ in range(3))
        changes = [None, None]
        inj = call(functools.partial(inject_kernel, step=step, steps=length),
                   (*marks, mat if block == 0 else token), (tiles(length, 8), tiles(length, 8)), 1 << 24)
        for field in range(2):
            for n, side in enumerate(order):
                first = block == 0
                if block == 1 and field == 0:
                    edge = call(edge_kernel, (keep[side], beyond[0][side]), quarter, 1 << 16)
                    vels[side] = [(vel, (0, 16)), (edge, (16 if side else -4, 4))]
                reach = 4 * length
                now_list = [(beyond[field][side], (16 if side else -reach, reach)), (now[field][0], (0, 8)), (now[field][1], (8, 8))]
                prev_list = [(prev_rows, None)] if first else prev[field]
                mid_list = []
                if length == 2:
                    mid_at = (4, 16) if side and n == 0 else (-4, 16) if n == 0 else (12, 8) if side else (-4, 8)
                    mid_list = [(None, mid_at)] + ([mids[field][order[0]]] if n == 1 else [])
                args = [keep[side], mat, inj[field]] + [a for a, _ in vels[side]]
                args += [a for a, _ in now_list] + [a for a, _ in prev_list] + [a for a, _ in mid_list[1:]]
                aliases = {}
                if field == 1:
                    args += [changes[side], image]
                    aliases = {len(args) - 1: 1}
                args.append(token)
                seen = (12 if n == 0 else 4) if length == 2 else 0
                ride = first and field == 0
                send = to_send == 4
                outs = [tiles(12) if ride else half, tiles(seen + 8) if field == 0 else tiles(16)]
                if length == 2:
                    outs.append(tiles(mid_at[1]))
                if send:
                    outs.append(quarter)
                out, extra, *rest = call(
                    functools.partial(
                        half_kernel, side=side, field=field, now_at=[at for _, at in now_list],
                        prev_at=None if first else [at for _, at in prev_list], vel_at=[at for _, at in vels[side]],
                        mid_at=[at for _, at in mid_list], masked=first, ride=ride, send=send),
                    args, outs, 1 << 25,
                    scratch=(pltpu.VMEM((2, 4, 8, 8, NY), F32), pltpu.VMEM((8, 8, 8, NY), F32)), aliases=aliases)
                token = out
                news[field][side] = out
                if length == 2:
                    mids[field][side] = (rest[0], mid_at)
                if field == 0:
                    changes[side] = extra
                else:
                    image = extra
                if not final:
                    sent[field][1 - side] = lax.ppermute(rest[-1] if send else out, "slab", up if side else down)
        if first:
            prev = [[(a, (0, 8)), (b, (8, 8)), (beyond[f][0], (-4, 4)), (beyond[f][1], (16, 4))] for f, (a, b) in enumerate(now)]
        else:
            prev = mids
        before_last, now, beyond = now, news, sent
        step += length

    terms, factor = call(terms_kernel, (image, vel_rows), (rows_of(shots * 64), rows_of(64)), 1 << 20)
    terms = lax.all_to_all(terms.reshape(shots, 64, NY), "shot", 0, 0, tiled=True)
    args = []
    for field in range(2):
        args += [*before_last[field], *now[field]]
    before, after = call(close_kernel, args, (rows_of(2 * PLANES * NX), rows_of(2 * PLANES * NX)), 1 << 22)
    gradient = call(sum_kernel, (terms.reshape(shots * 64, NY), factor), rows_of(64), 1 << 18).reshape(velocity.shape)
    shape = fields_now.shape
    return gradient, before.reshape(shape), after.reshape(shape)


def solution(mesh):
    return jax.shard_map(
        body,
        mesh=mesh,
        in_specs=(
            P("slab", "shot", None),
            P("shot", None, "slab", None, None),
            P("shot", None, "slab", None, None),
            P("shot", "slab"),
            P("shot", None, "slab"),
            P("shot", "slab"),
            P("shot", None, "slab"),
        ),
        out_specs=(
            P("slab", "shot", None),
            P("shot", None, "slab", None, None),
            P("shot", None, "slab", None, None),
        ),
        check_vma=False,
    )
```

```python
import functools

import jax
import jax.numpy as jnp
from jax import lax
from jax.experimental import pallas as pl
from jax.experimental.pallas import tpu as pltpu
from jax.sharding import PartitionSpec as P

STEPS = 8
PLANES = 16
NX = 64
NY = 128
SCALE = 5040.0
TAPS = (8064.0, -1008.0, 128.0, -9.0)
CENTRE = (-43008.0, -42.0)
F32 = jnp.float32
BF16 = jnp.bfloat16
VMEM_LIMIT = 16 * 1024 * 1024


def fill_x_matrix(mat_ref):
    row = lax.broadcasted_iota(jnp.int32, (NX, 4 * NX), 0)
    col = lax.broadcasted_iota(jnp.int32, (NX, 4 * NX), 1)
    place = lambda n: (n & 7) * 8 + ((n & (NX - 1)) >> 3)
    apart = jnp.abs(place(row) - place(col))
    first = jnp.where(apart == 0, CENTRE[0], 0.0)
    for reach, tap in enumerate(TAPS, 1):
        first = jnp.where(apart == reach, tap, first)
    second = jnp.where(apart == 0, CENTRE[1], 0.0)
    mat_ref[...] = jnp.where(col < 2 * NX, first, second).astype(BF16)


def fill_matrix(mat_ref):
    row = lax.broadcasted_iota(jnp.int32, (2 * NY, NY), 0)
    col = lax.broadcasted_iota(jnp.int32, (2 * NY, NY), 1)
    apart = jnp.abs((row & (NY - 1)) - col)
    out = jnp.zeros((2 * NY, NY), F32)
    for reach, tap in enumerate(TAPS, 1):
        out = jnp.where(apart == reach, tap, out)
    mat_ref[...] = out.astype(BF16)


class Rows:
    def __init__(self, *parts):
        self.parts = parts

    def find(self, plane):
        for ref, first, count in self.parts:
            if first <= plane < first + count:
                return ref, plane - first
        raise ValueError(plane)

    def tile(self, plane, j):
        ref, at = self.find(plane)
        return ref[at, j]

    def chunk(self, plane, count):
        ref, at = self.find(plane)
        return ref[pl.ds(at, count)]

    def put(self, plane, j, value):
        ref, at = self.find(plane)
        ref[at, j] = value


def advance(src, prev, dest, vel, first, mat_ref, x_ref, part, inj, see):
    rows = src.chunk(first, 4).reshape(4 * NX, NY)
    high = rows.astype(BF16)
    low = (rows - high.astype(F32)).astype(BF16)
    both = jnp.concatenate([high, low], axis=1)
    along_y = jnp.dot(both, mat_ref[...], preferred_element_type=F32)
    for p in (0, 2):
        sides = []
        for at in (p * NX, (p + 1) * NX):
            sides.append(jnp.concatenate([high[at:at + NX], low[at:at + NX]] * 2, axis=0))
        along_x = jnp.dot(x_ref[...], jnp.concatenate(sides, axis=1), preferred_element_type=F32)
        for q in range(2):
            at = (p + q) * NX
            part[p + q] = (along_y[at:at + NX] + along_x[:, q * NY:(q + 1) * NY]).reshape(8, 8, NY)
    for p in range(4):
        plane = first + p
        for j in range(8):
            here = src.tile(plane, j)
            total = part[p, j]
            for reach, tap in enumerate(TAPS, 1):
                total = total + tap * (src.tile(plane + reach, j) + src.tile(plane - reach, j))
            change = vel.tile(plane, j) * total
            if 4 <= plane < 12:
                change = change + inj[plane - 4, j]
            dest.put(plane, j, (here + here) - prev.tile(plane, j) + change)
            if 0 <= plane < PLANES:
                see(plane, j, change, here)


class Natural:
    def __init__(self, ref, field):
        self.ref, self.field = ref, field

    def tile(self, plane, j):
        return self.ref[pl.ds((self.field * PLANES + plane) * NX + j, 8, stride=8), :]


def half_kernel(*refs, side, field, now_at, prev_at, vel_at, mid_at, masked, ride, send):
    refs = list(refs)
    take = lambda count: [refs.pop(0) for _ in range(count)]
    rows = lambda some, at: Rows(*[(ref, *where) for ref, where in zip(some, at)])
    keep, mat_ref, x_ref, inj = take(4)
    vel = rows(take(len(vel_at)), vel_at)
    now_refs = take(len(now_at))
    prev = Natural(take(1)[0], field) if prev_at is None else rows(take(len(prev_at)), prev_at)
    other_mid = take(max(len(mid_at) - 1, 0))
    if field == 1:
        changes, image_in = take(2)
        del image_in
    take(1)
    out, extra = take(2)
    mid = take(1) if mid_at else []
    message = take(1)[0] if send else None
    part, beyond = refs
    if masked:
        beyond = now_refs[0]
    else:
        inside = keep[...] > 0.0
        for p in range(now_at[0][1]):
            for j in range(8):
                beyond[p, j] = jnp.where(inside, now_refs[0][p, j], 0.0)
    now = rows([beyond, *now_refs[1:]], now_at)
    base = 8 * side
    last = Rows((out, base, 8))
    if mid_at:
        mids = rows([*mid, *other_mid], mid_at)
        starts = range(mid_at[0][0], sum(mid_at[0]), 4)
        seen = [p for p in range(mid_at[0][0], sum(mid_at[0])) if 0 <= p < PLANES]

    def see(first):
        def change_out(plane, j, change, here):
            extra[plane - first, j] = change

        def image_out(plane, j, change, here):
            extra[plane, j] += changes[plane - first, j] * here

        return change_out if field == 0 else image_out

    run = functools.partial(advance, vel=vel, mat_ref=mat_ref, x_ref=x_ref)
    skip = 0
    if mid_at:
        for n, lo in enumerate(starts):
            run(now, prev, mids, first=lo, part=part.at[n % 2], inj=inj.at[0], see=see(seen[0]))
        now, prev, skip = mids, now, len(seen)
    for n, lo in enumerate((base, base + 4)):
        run(now, prev, last, first=lo, part=part.at[n % 2], inj=inj.at[1 if mid_at else 0], see=see(base - skip))
    border = 12 if side else 0
    for p in range(4):
        for j in range(8):
            if ride:
                out[8 + p, j] = vel.tile(border + p, j)
            if send:
                message[p, j] = out[border - base + p, j]


def edge_kernel(keep, message, out):
    inside = keep[...] > 0.0
    for p in range(4):
        for j in range(8):
            out[p, j] = jnp.where(inside, message[8 + p, j], 0.0)


def pack_kernel(now_in, up_msg, down_msg, low_0, high_0, low_1, high_1, mat_ref, x_ref):
    fill_matrix(mat_ref)
    fill_x_matrix(x_ref)
    for field, (low, high) in enumerate(((low_0, high_0), (low_1, high_1))):
        now = Natural(now_in, field)
        for p in range(PLANES):
            for j in range(8):
                tile = now.tile(p, j)
                (high if p >= 8 else low)[p % 8, j] = tile
                if p < 4:
                    down_msg[field, p, j] = tile
                if p >= 12:
                    up_msg[field, p - 12, j] = tile


def spread_kernel(own, out, factor):
    speed = own[...]
    factor[...] = (-2.0 / (16 * STEPS)) / (speed * speed * speed)
    for shot in range(16):
        out[pl.ds(shot * 64, 64), :] = own[...]


def dense(cells, amps, step, steps):
    count = cells.shape[1]
    cell = cells[...]
    z, x, y = cell >> 13, (cell >> 7) & (NX - 1), cell & (NY - 1)
    row = (z - 4) * NX + (x & 7) * 8 + (x >> 3)
    hit = (lax.broadcasted_iota(jnp.int32, (8 * NX, count), 0) == row).astype(F32).astype(BF16)
    hits = jnp.concatenate([hit, hit, hit], axis=1)
    lane = lax.broadcasted_iota(jnp.int32, (NY, count), 0) == y
    sides = []
    for at in range(step, step + steps):
        amount = amps[pl.ds(at, 1), :]
        high = amount.astype(BF16).astype(F32)
        rest = amount - high
        middle = rest.astype(BF16).astype(F32)
        low = rest - middle
        sides.append(jnp.concatenate([jnp.where(lane, part, 0.0).astype(BF16) for part in (high, middle, low)], axis=1))
    both = jnp.concatenate(sides, axis=0)
    return lax.dot_general(hits, both, (((1,), (1,)), ((), ())), preferred_element_type=F32)


def inject_kernel(source_cells, source_amps, cells, amps, token, out_0, out_1, *, step, steps):
    del token
    values = dense(cells, amps, step, steps)
    for at in range(steps):
        out_1[at] = values[:, at * NY:(at + 1) * NY].reshape(8, 8, 8, NY)

    def pick(array, row, column):
        spot = (lax.broadcasted_iota(jnp.int32, array.shape, 0) == row) & (lax.broadcasted_iota(jnp.int32, array.shape, 1) == column)
        return jnp.sum(jnp.where(spot, array, 0.0), keepdims=True)

    sub = lax.broadcasted_iota(jnp.int32, (8, NY), 0)
    lane = lax.broadcasted_iota(jnp.int32, (8, NY), 1)
    places = source_cells[...].astype(F32)
    count = source_cells.shape[1]
    rows, columns, amounts = [], [], []
    for n in range(count):
        cell = pick(places, 0, n).astype(jnp.int32)
        z, x, y = cell >> 13, (cell >> 7) & (NX - 1), cell & (NY - 1)
        rows.append(sub - ((z - 4) * NX + (x & 7) * 8 + (x >> 3)))
        columns.append(lane == y)
        amounts.append([pick(source_amps[...], n, step + at) for at in range(steps)])
    for p in range(8):
        for j in range(8):
            hits = [(row == -(p * NX + j * 8)) & column for row, column in zip(rows, columns)]
            for at in range(steps):
                total = jnp.zeros((8, NY), F32)
                for hit, amount in zip(hits, amounts):
                    total = total + jnp.where(hit, amount[at], 0.0)
                out_0[at, p, j] = total


def open_kernel(keep_below, keep_above, gathered, below, above,
                vel, image, below_out_0, above_out_0, below_out_1, above_out_1):
    image[...] = jnp.zeros_like(image)
    for p in range(PLANES):
        for j in range(8):
            line = gathered[pl.ds((j // 4) * 64 + p * 4 + j % 4, 8, stride=128), :]
            vel[p, j] = line * line * (1.0 / SCALE)
    for keep, src, dests in ((keep_below, below, (below_out_0, below_out_1)), (keep_above, above, (above_out_0, above_out_1))):
        inside = keep[...] > 0.0
        for field, dest in enumerate(dests):
            for p in range(4):
                for j in range(8):
                    dest[p, j] = jnp.where(inside, src[field, p, j], 0.0)


def terms_kernel(image, out):
    for p in range(PLANES):
        for j in range(8):
            out[pl.ds((j // 4) * 64 + p * 4 + j % 4, 8, stride=128), :] = image[p, j]


def sum_kernel(terms, factor, out):
    total = terms[0:64, :]
    for shot in range(1, 16):
        total = total + terms[pl.ds(64 * shot, 64), :]
    out[...] = total * factor[...]


def close_kernel(before_low_0, before_high_0, low_0, high_0, before_low_1, before_high_1, low_1, high_1, before, after):
    for field, (before_low, before_high, low, high) in enumerate(
            ((before_low_0, before_high_0, low_0, high_0), (before_low_1, before_high_1, low_1, high_1))):
        for p in range(PLANES):
            for j in range(8):
                rows = pl.ds((field * PLANES + p) * NX + j, 8, stride=8)
                before[rows, :] = (before_high if p >= 8 else before_low)[p % 8, j]
                after[rows, :] = (high if p >= 8 else low)[p % 8, j]


def tiles(*lead):
    return jax.ShapeDtypeStruct((*lead, 8, 8, NY), F32)


def rows_of(count):
    return jax.ShapeDtypeStruct((count, NY), F32)


def call(kernel, args, outs, flops, scratch=(), aliases=None):
    whole = pl.BlockSpec(memory_space=pltpu.VMEM)
    return pl.pallas_call(
        kernel,
        in_specs=[whole] * len(args),
        out_specs=jax.tree.map(lambda _: whole, outs),
        out_shape=outs,
        scratch_shapes=list(scratch),
        input_output_aliases=aliases or {},
        compiler_params=pltpu.CompilerParams(vmem_limit_bytes=VMEM_LIMIT),
        cost_estimate=pl.CostEstimate(flops=flops, bytes_accessed=1 << 20, transcendentals=0),
    )(*args)


def body(
    velocity, fields_prev, fields_now, source_cells, source_traces, receiver_cells, receiver_traces
):
    slabs, shots = lax.axis_size("slab"), lax.axis_size("shot")
    up = [(i, (i + 1) % slabs) for i in range(slabs)]
    down = [(j, i) for i, j in up]
    slab = lax.axis_index("slab")
    keep = [jnp.full((8, NY), slab > 0, F32), jnp.full((8, NY), slab < slabs - 1, F32)]

    vel_rows = velocity.reshape(PLANES * 4, NY)
    spread, factor = call(spread_kernel, (vel_rows,), (rows_of(shots * 64), rows_of(64)), 1 << 20)
    gathered = lax.all_to_all(spread.reshape(shots, 64, NY), "shot", 0, 0, tiled=True)
    half, quarter = tiles(8), tiles(4)
    mat, mat_x = jax.ShapeDtypeStruct((2 * NY, NY), BF16), jax.ShapeDtypeStruct((NX, 4 * NX), BF16)
    up_msg, down_msg, low_0, high_0, low_1, high_1, mat, mat_x = call(
        pack_kernel, (fields_now.reshape(-1, NY),), (*[tiles(2, 4)] * 2, *[half] * 4, mat, mat_x), 1 << 22)
    now = [[low_0, high_0], [low_1, high_1]]
    arrived = [lax.ppermute(up_msg, "slab", up), lax.ppermute(down_msg, "slab", down)]
    marks = (source_cells, source_traces[0].T, receiver_cells, receiver_traces[0])
    vel, image, *far = call(
        open_kernel, (*keep, gathered.reshape(shots * 64, NY), *arrived), (tiles(16), tiles(16), *[quarter] * 4), 1 << 22)
    beyond = [far[:2], far[2:]]
    vels = [[(vel, (0, 16))], [(vel, (0, 16))]]
    prev_rows = fields_prev.reshape(-1, NY)

    lengths = (1, 2, 2, 2, 1)
    token, step, prev = image, 0, None
    for block, length in enumerate(lengths):
        final = block == len(lengths) - 1
        to_send = 0 if final else 4 * lengths[block + 1]
        order = (1, 0) if block % 2 == 0 else (0, 1)
        first = block == 0
        news, mids, sent = ([[None, None], [None, None]] for _ in range(3))
        changes = [None, None]
        inj = call(functools.partial(inject_kernel, step=step, steps=length),
                   (*marks, mat if block == 0 else token), (tiles(length, 8), tiles(length, 8)), 1 << 24)
        for field in range(2):
            for n, side in enumerate(order):
                if block == 1 and field == 0:
                    edge = call(edge_kernel, (keep[side], beyond[0][side]), quarter, 1 << 16)
                    vels[side] = [(vel, (0, 16)), (edge, (16 if side else -4, 4))]
                reach = 4 * length
                now_list = [(beyond[field][side], (16 if side else -reach, reach)), (now[field][0], (0, 8)), (now[field][1], (8, 8))]
                prev_list = [(prev_rows, None)] if first else prev[field]
                mid_list = []
                if length == 2:
                    mid_at = (4, 16) if side and n == 0 else (-4, 16) if n == 0 else (12, 8) if side else (-4, 8)
                    mid_list = [(None, mid_at)] + ([mids[field][order[0]]] if n == 1 else [])
                args = [keep[side], mat, mat_x, inj[field]] + [a for a, _ in vels[side]]
                args += [a for a, _ in now_list] + [a for a, _ in prev_list] + [a for a, _ in mid_list[1:]]
                aliases = {}
                if field == 1:
                    args += [changes[side], image]
                    aliases = {len(args) - 1: 1}
                args.append(token)
                seen = (12 if n == 0 else 4) if length == 2 else 0
                ride = first and field == 0
                send = to_send == 4
                outs = [tiles(12) if ride else half, tiles(seen + 8) if field == 0 else tiles(16)]
                if length == 2:
                    outs.append(tiles(mid_at[1]))
                if send:
                    outs.append(quarter)
                out, extra, *rest = call(
                    functools.partial(
                        half_kernel, side=side, field=field, now_at=[at for _, at in now_list],
                        prev_at=None if first else [at for _, at in prev_list], vel_at=[at for _, at in vels[side]],
                        mid_at=[at for _, at in mid_list], masked=first, ride=ride, send=send),
                    args, outs, 1 << 25,
                    scratch=(pltpu.VMEM((2, 4, 8, 8, NY), F32), pltpu.VMEM((8, 8, 8, NY), F32)), aliases=aliases)
                token = out
                news[field][side] = out
                if length == 2:
                    mids[field][side] = (rest[0], mid_at)
                if field == 0:
                    changes[side] = extra
                else:
                    image = extra
                if not final:
                    sent[field][1 - side] = lax.ppermute(rest[-1] if send else out, "slab", up if side else down)
        if first:
            prev = [[(a, (0, 8)), (b, (8, 8)), (beyond[f][0], (-4, 4)), (beyond[f][1], (16, 4))] for f, (a, b) in enumerate(now)]
        else:
            prev = mids
        before_last, now, beyond = now, news, sent
        step += length

    terms = call(terms_kernel, (image,), rows_of(shots * 64), 1 << 20)
    terms = lax.all_to_all(terms.reshape(shots, 64, NY), "shot", 0, 0, tiled=True)
    args = []
    for field in range(2):
        args += [*before_last[field], *now[field]]
    before, after = call(close_kernel, args, (rows_of(2 * PLANES * NX), rows_of(2 * PLANES * NX)), 1 << 22)
    gradient = call(sum_kernel, (terms.reshape(shots * 64, NY), factor), rows_of(64), 1 << 18).reshape(velocity.shape)
    shape = fields_now.shape
    return gradient, before.reshape(shape), after.reshape(shape)


def solution(mesh):
    return jax.shard_map(
        body,
        mesh=mesh,
        in_specs=(
            P("slab", "shot", None),
            P("shot", None, "slab", None, None),
            P("shot", None, "slab", None, None),
            P("shot", "slab"),
            P("shot", None, "slab"),
            P("shot", "slab"),
            P("shot", None, "slab"),
        ),
        out_specs=(
            P("slab", "shot", None),
            P("shot", None, "slab", None, None),
            P("shot", None, "slab", None, None),
        ),
        check_vma=False,
    )
```

```python
import functools

import jax
import jax.numpy as jnp
from jax import lax
from jax.experimental import pallas as pl
from jax.experimental.pallas import tpu as pltpu
from jax.sharding import PartitionSpec as P

STEPS = 8
PLANES = 16
NX = 64
NY = 128
SCALE = 5040.0
TAPS = (8064.0, -1008.0, 128.0, -9.0)
CENTRE = (-43008.0, -42.0)
F32 = jnp.float32
BF16 = jnp.bfloat16
VMEM_LIMIT = 16 * 1024 * 1024


def fill_x_matrix(mat_ref):
    row = lax.broadcasted_iota(jnp.int32, (NX, 4 * NX), 0)
    col = lax.broadcasted_iota(jnp.int32, (NX, 4 * NX), 1)
    place = lambda n: (n & 7) * 8 + ((n & (NX - 1)) >> 3)
    apart = jnp.abs(place(row) - place(col))
    first = jnp.where(apart == 0, CENTRE[0], 0.0)
    for reach, tap in enumerate(TAPS, 1):
        first = jnp.where(apart == reach, tap, first)
    second = jnp.where(apart == 0, CENTRE[1], 0.0)
    mat_ref[...] = jnp.where(col < 2 * NX, first, second).astype(BF16)


def fill_matrix(mat_ref):
    row = lax.broadcasted_iota(jnp.int32, (2 * NY, NY), 0)
    col = lax.broadcasted_iota(jnp.int32, (2 * NY, NY), 1)
    apart = jnp.abs((row & (NY - 1)) - col)
    out = jnp.zeros((2 * NY, NY), F32)
    for reach, tap in enumerate(TAPS, 1):
        out = jnp.where(apart == reach, tap, out)
    mat_ref[...] = out.astype(BF16)


class Rows:
    def __init__(self, *parts):
        self.parts = parts

    def find(self, plane):
        for ref, first, count in self.parts:
            if first <= plane < first + count:
                return ref, plane - first
        raise ValueError(plane)

    def tile(self, plane, j):
        ref, at = self.find(plane)
        return ref[at, j]

    def chunk(self, plane, count):
        ref, at = self.find(plane)
        return ref[pl.ds(at, count)]

    def put(self, plane, j, value):
        ref, at = self.find(plane)
        ref[at, j] = value


def advance(src, prev, dest, vel, first, mat_ref, x_ref, part, inj, see):
    rows = src.chunk(first, 4).reshape(4 * NX, NY)
    high = rows.astype(BF16)
    low = (rows - high.astype(F32)).astype(BF16)
    both = jnp.concatenate([high, low], axis=1)
    along_y = jnp.dot(both, mat_ref[...], preferred_element_type=F32)
    for p in (0, 2):
        sides = []
        for at in (p * NX, (p + 1) * NX):
            sides.append(jnp.concatenate([high[at:at + NX], low[at:at + NX]] * 2, axis=0))
        along_x = jnp.dot(x_ref[...], jnp.concatenate(sides, axis=1), preferred_element_type=F32)
        for q in range(2):
            at = (p + q) * NX
            part[p + q] = (along_y[at:at + NX] + along_x[:, q * NY:(q + 1) * NY]).reshape(8, 8, NY)
    for p in range(4):
        plane = first + p
        for j in range(8):
            here = src.tile(plane, j)
            total = part[p, j]
            for reach, tap in enumerate(TAPS, 1):
                total = total + tap * (src.tile(plane + reach, j) + src.tile(plane - reach, j))
            change = vel.tile(plane, j) * total
            if 4 <= plane < 12:
                change = change + inj[plane - 4, j]
            dest.put(plane, j, (here + here) - prev.tile(plane, j) + change)
            if 0 <= plane < PLANES:
                see(plane, j, change, here)


class Natural:
    def __init__(self, ref, field):
        self.ref, self.field = ref, field

    def tile(self, plane, j):
        return self.ref[pl.ds((self.field * PLANES + plane) * NX + j, 8, stride=8), :]


def half_kernel(*refs, side, field, now_at, prev_at, vel_at, mid_at, masked, ride, send):
    refs = list(refs)
    take = lambda count: [refs.pop(0) for _ in range(count)]
    rows = lambda some, at: Rows(*[(ref, *where) for ref, where in zip(some, at)])
    keep, mat_ref, x_ref, inj = take(4)
    vel = rows(take(len(vel_at)), vel_at)
    now_refs = take(len(now_at))
    prev = Natural(take(1)[0], field) if prev_at is None else rows(take(len(prev_at)), prev_at)
    other_mid = take(max(len(mid_at) - 1, 0))
    if field == 1:
        changes, image_in = take(2)
        del image_in
    take(1)
    out, extra = take(2)
    mid = take(1) if mid_at else []
    message = take(1)[0] if send else None
    part, beyond = refs
    if masked:
        beyond = now_refs[0]
    else:
        inside = keep[...] > 0.0
        for p in range(now_at[0][1]):
            for j in range(8):
                beyond[p, j] = jnp.where(inside, now_refs[0][p, j], 0.0)
    now = rows([beyond, *now_refs[1:]], now_at)
    base = 8 * side
    last = Rows((out, base, 8))
    if mid_at:
        mids = rows([*mid, *other_mid], mid_at)
        starts = range(mid_at[0][0], sum(mid_at[0]), 4)
        seen = [p for p in range(mid_at[0][0], sum(mid_at[0])) if 0 <= p < PLANES]

    def see(first):
        def change_out(plane, j, change, here):
            extra[plane - first, j] = change

        def image_out(plane, j, change, here):
            extra[plane, j] += changes[plane - first, j] * here

        return change_out if field == 0 else image_out

    run = functools.partial(advance, vel=vel, mat_ref=mat_ref, x_ref=x_ref)
    skip = 0
    if mid_at:
        for n, lo in enumerate(starts):
            run(now, prev, mids, first=lo, part=part.at[n % 2], inj=inj.at[0], see=see(seen[0]))
        now, prev, skip = mids, now, len(seen)
    for n, lo in enumerate((base, base + 4)):
        run(now, prev, last, first=lo, part=part.at[n % 2], inj=inj.at[1 if mid_at else 0], see=see(base - skip))
    border = 12 if side else 0
    for p in range(4):
        for j in range(8):
            if ride:
                out[8 + p, j] = vel.tile(border + p, j)
            if send:
                message[p, j] = out[border - base + p, j]


def edge_kernel(keep, message, out):
    inside = keep[...] > 0.0
    for p in range(4):
        for j in range(8):
            out[p, j] = jnp.where(inside, message[8 + p, j], 0.0)


def pack_kernel(now_in, up_msg, down_msg, low_0, high_0, low_1, high_1, mat_ref, x_ref):
    fill_matrix(mat_ref)
    fill_x_matrix(x_ref)
    for field, (low, high) in enumerate(((low_0, high_0), (low_1, high_1))):
        now = Natural(now_in, field)
        for p in range(PLANES):
            for j in range(8):
                tile = now.tile(p, j)
                (high if p >= 8 else low)[p % 8, j] = tile
                if p < 4:
                    down_msg[field, p, j] = tile
                if p >= 12:
                    up_msg[field, p - 12, j] = tile


def spread_kernel(own, out, factor):
    speed = own[...]
    factor[...] = (-2.0 / (16 * STEPS)) / (speed * speed * speed)
    for shot in range(16):
        out[pl.ds(shot * 64, 64), :] = own[...]


def dense(cells, amps, step, steps):
    count = cells.shape[1]
    cell = cells[...]
    z, x, y = cell >> 13, (cell >> 7) & (NX - 1), cell & (NY - 1)
    row = (z - 4) * NX + (x & 7) * 8 + (x >> 3)
    hit = (lax.broadcasted_iota(jnp.int32, (8 * NX, count), 0) == row).astype(F32).astype(BF16)
    hits = jnp.concatenate([hit, hit, hit], axis=1)
    lane = lax.broadcasted_iota(jnp.int32, (NY, count), 0) == y
    sides = []
    for at in range(step, step + steps):
        amount = amps[pl.ds(at, 1), :]
        high = amount.astype(BF16).astype(F32)
        rest = amount - high
        middle = rest.astype(BF16).astype(F32)
        low = rest - middle
        sides.append(jnp.concatenate([jnp.where(lane, part, 0.0).astype(BF16) for part in (high, middle, low)], axis=1))
    both = jnp.concatenate(sides, axis=0)
    return lax.dot_general(hits, both, (((1,), (1,)), ((), ())), preferred_element_type=F32)


def inject_kernel(source_cells, source_amps, cells, amps, token, out_0, out_1, *, step, steps):
    del token
    values = dense(cells, amps, step, steps)
    for at in range(steps):
        out_1[at] = values[:, at * NY:(at + 1) * NY].reshape(8, 8, 8, NY)

    def pick(array, row, column):
        spot = (lax.broadcasted_iota(jnp.int32, array.shape, 0) == row) & (lax.broadcasted_iota(jnp.int32, array.shape, 1) == column)
        return jnp.sum(jnp.where(spot, array, 0.0), keepdims=True)

    sub = lax.broadcasted_iota(jnp.int32, (8, NY), 0)
    lane = lax.broadcasted_iota(jnp.int32, (8, NY), 1)
    places = source_cells[...].astype(F32)
    count = source_cells.shape[1]
    rows, columns, amounts = [], [], []
    for n in range(count):
        cell = pick(places, 0, n).astype(jnp.int32)
        z, x, y = cell >> 13, (cell >> 7) & (NX - 1), cell & (NY - 1)
        rows.append(sub - ((z - 4) * NX + (x & 7) * 8 + (x >> 3)))
        columns.append(lane == y)
        amounts.append([pick(source_amps[...], n, step + at) for at in range(steps)])
    for p in range(8):
        for j in range(8):
            hits = [(row == -(p * NX + j * 8)) & column for row, column in zip(rows, columns)]
            for at in range(steps):
                total = jnp.zeros((8, NY), F32)
                for hit, amount in zip(hits, amounts):
                    total = total + jnp.where(hit, amount[at], 0.0)
                out_0[at, p, j] = total


def open_kernel(keep_below, keep_above, gathered, below, above,
                vel, image, below_out_0, above_out_0, below_out_1, above_out_1):
    image[...] = jnp.zeros_like(image)
    for p in range(PLANES):
        for j in range(8):
            line = gathered[pl.ds((j // 4) * 64 + p * 4 + j % 4, 8, stride=128), :]
            vel[p, j] = line * line * (1.0 / SCALE)
    for keep, src, dests in ((keep_below, below, (below_out_0, below_out_1)), (keep_above, above, (above_out_0, above_out_1))):
        inside = keep[...] > 0.0
        for field, dest in enumerate(dests):
            for p in range(4):
                for j in range(8):
                    dest[p, j] = jnp.where(inside, src[field, p, j], 0.0)


def terms_kernel(image, out):
    for p in range(PLANES):
        for j in range(8):
            out[pl.ds((j // 4) * 64 + p * 4 + j % 4, 8, stride=128), :] = image[p, j]


def sum_kernel(terms, factor, out):
    total = terms[0:64, :]
    for shot in range(1, 16):
        total = total + terms[pl.ds(64 * shot, 64), :]
    out[...] = total * factor[...]


def close_kernel(before_low_0, before_high_0, low_0, high_0, before_low_1, before_high_1, low_1, high_1, before, after):
    for field, (before_low, before_high, low, high) in enumerate(
            ((before_low_0, before_high_0, low_0, high_0), (before_low_1, before_high_1, low_1, high_1))):
        for p in range(PLANES):
            for j in range(8):
                rows = pl.ds((field * PLANES + p) * NX + j, 8, stride=8)
                before[rows, :] = (before_high if p >= 8 else before_low)[p % 8, j]
                after[rows, :] = (high if p >= 8 else low)[p % 8, j]


def tiles(*lead):
    return jax.ShapeDtypeStruct((*lead, 8, 8, NY), F32)


def rows_of(count):
    return jax.ShapeDtypeStruct((count, NY), F32)


def call(kernel, args, outs, flops, scratch=(), aliases=None):
    whole = pl.BlockSpec(memory_space=pltpu.VMEM)
    return pl.pallas_call(
        kernel,
        in_specs=[whole] * len(args),
        out_specs=jax.tree.map(lambda _: whole, outs),
        out_shape=outs,
        scratch_shapes=list(scratch),
        input_output_aliases=aliases or {},
        compiler_params=pltpu.CompilerParams(vmem_limit_bytes=VMEM_LIMIT),
        cost_estimate=pl.CostEstimate(flops=flops, bytes_accessed=1 << 20, transcendentals=0),
    )(*args)


def body(
    velocity, fields_prev, fields_now, source_cells, source_traces, receiver_cells, receiver_traces
):
    slabs, shots = lax.axis_size("slab"), lax.axis_size("shot")
    up = [(i, (i + 1) % slabs) for i in range(slabs)]
    down = [(j, i) for i, j in up]
    slab = lax.axis_index("slab")
    keep = [jnp.full((8, NY), slab > 0, F32), jnp.full((8, NY), slab < slabs - 1, F32)]

    vel_rows = velocity.reshape(PLANES * 4, NY)
    spread, factor = call(spread_kernel, (vel_rows,), (rows_of(shots * 64), rows_of(64)), 1 << 20)
    gathered = lax.all_to_all(spread.reshape(shots, 64, NY), "shot", 0, 0, tiled=True)
    half, quarter = tiles(8), tiles(4)
    mat, mat_x = jax.ShapeDtypeStruct((2 * NY, NY), BF16), jax.ShapeDtypeStruct((NX, 4 * NX), BF16)
    up_msg, down_msg, low_0, high_0, low_1, high_1, mat, mat_x = call(
        pack_kernel, (fields_now.reshape(-1, NY),), (*[tiles(2, 4)] * 2, *[half] * 4, mat, mat_x), 1 << 22)
    now = [[low_0, high_0], [low_1, high_1]]
    arrived = [lax.ppermute(up_msg, "slab", up), lax.ppermute(down_msg, "slab", down)]
    marks = (source_cells, source_traces[0].T, receiver_cells, receiver_traces[0])
    vel, image, *far = call(
        open_kernel, (*keep, gathered.reshape(shots * 64, NY), *arrived), (tiles(16), tiles(16), *[quarter] * 4), 1 << 22)
    beyond = [far[:2], far[2:]]
    vels = [[(vel, (0, 16))], [(vel, (0, 16))]]
    prev_rows = fields_prev.reshape(-1, NY)

    lengths = (1, 2, 2, 2, 1)
    token, step, prev = image, 0, None
    for block, length in enumerate(lengths):
        final = block == len(lengths) - 1
        to_send = 0 if final else 4 * lengths[block + 1]
        order = (1, 0) if block % 2 == 0 else (0, 1)
        first = block == 0
        news, mids, sent = ([[None, None], [None, None]] for _ in range(3))
        changes = [None, None]
        inj = call(functools.partial(inject_kernel, step=step, steps=length),
                   (*marks, mat if block == 0 else token), (tiles(length, 8), tiles(length, 8)), 1 << 24)
        walk = [(f, n) for f in range(2) for n in range(2)] if length == 2 else [(f, n) for n in range(2) for f in range(2)]
        for field, n in walk:
            if True:
                side = order[n]
                if block == 1 and field == 0:
                    edge = call(edge_kernel, (keep[side], beyond[0][side]), quarter, 1 << 16)
                    vels[side] = [(vel, (0, 16)), (edge, (16 if side else -4, 4))]
                reach = 4 * length
                now_list = [(beyond[field][side], (16 if side else -reach, reach)), (now[field][0], (0, 8)), (now[field][1], (8, 8))]
                prev_list = [(prev_rows, None)] if first else prev[field]
                mid_list = []
                if length == 2:
                    mid_at = (4, 16) if side and n == 0 else (-4, 16) if n == 0 else (12, 8) if side else (-4, 8)
                    mid_list = [(None, mid_at)] + ([mids[field][order[0]]] if n == 1 else [])
                args = [keep[side], mat, mat_x, inj[field]] + [a for a, _ in vels[side]]
                args += [a for a, _ in now_list] + [a for a, _ in prev_list] + [a for a, _ in mid_list[1:]]
                aliases = {}
                if field == 1:
                    args += [changes[side], image]
                    aliases = {len(args) - 1: 1}
                args.append(token)
                seen = (12 if n == 0 else 4) if length == 2 else 0
                ride = first and field == 0
                send = to_send == 4
                outs = [tiles(12) if ride else half, tiles(seen + 8) if field == 0 else tiles(16)]
                if length == 2:
                    outs.append(tiles(mid_at[1]))
                if send:
                    outs.append(quarter)
                out, extra, *rest = call(
                    functools.partial(
                        half_kernel, side=side, field=field, now_at=[at for _, at in now_list],
                        prev_at=None if first else [at for _, at in prev_list], vel_at=[at for _, at in vels[side]],
                        mid_at=[at for _, at in mid_list], masked=first, ride=ride, send=send),
                    args, outs, 1 << 25,
                    scratch=(pltpu.VMEM((2, 4, 8, 8, NY), F32), pltpu.VMEM((8, 8, 8, NY), F32)), aliases=aliases)
                token = out
                news[field][side] = out
                if length == 2:
                    mids[field][side] = (rest[0], mid_at)
                if field == 0:
                    changes[side] = extra
                else:
                    image = extra
                if not final:
                    sent[field][1 - side] = lax.ppermute(rest[-1] if send else out, "slab", up if side else down)
        if first:
            prev = [[(a, (0, 8)), (b, (8, 8)), (beyond[f][0], (-4, 4)), (beyond[f][1], (16, 4))] for f, (a, b) in enumerate(now)]
        else:
            prev = mids
        before_last, now, beyond = now, news, sent
        step += length

    terms = call(terms_kernel, (image,), rows_of(shots * 64), 1 << 20)
    terms = lax.all_to_all(terms.reshape(shots, 64, NY), "shot", 0, 0, tiled=True)
    args = []
    for field in range(2):
        args += [*before_last[field], *now[field]]
    before, after = call(close_kernel, args, (rows_of(2 * PLANES * NX), rows_of(2 * PLANES * NX)), 1 << 22)
    gradient = call(sum_kernel, (terms.reshape(shots * 64, NY), factor), rows_of(64), 1 << 18).reshape(velocity.shape)
    shape = fields_now.shape
    return gradient, before.reshape(shape), after.reshape(shape)


def solution(mesh):
    return jax.shard_map(
        body,
        mesh=mesh,
        in_specs=(
            P("slab", "shot", None),
            P("shot", None, "slab", None, None),
            P("shot", None, "slab", None, None),
            P("shot", "slab"),
            P("shot", None, "slab"),
            P("shot", "slab"),
            P("shot", None, "slab"),
        ),
        out_specs=(
            P("slab", "shot", None),
            P("shot", None, "slab", None, None),
            P("shot", None, "slab", None, None),
        ),
        check_vma=False,
    )
```

```python
import functools

import jax
import jax.numpy as jnp
from jax import lax
from jax.experimental import pallas as pl
from jax.experimental.pallas import tpu as pltpu
from jax.sharding import PartitionSpec as P

STEPS = 8
PLANES = 16
NX = 64
NY = 128
SCALE = 5040.0
TAPS = (8064.0, -1008.0, 128.0, -9.0)
CENTRE = (-43008.0, -42.0)
F32 = jnp.float32
BF16 = jnp.bfloat16
VMEM_LIMIT = 16 * 1024 * 1024


def fill_x_matrix(mat_ref):
    row = lax.broadcasted_iota(jnp.int32, (NX, 4 * NX), 0)
    col = lax.broadcasted_iota(jnp.int32, (NX, 4 * NX), 1)
    place = lambda n: (n & 7) * 8 + ((n & (NX - 1)) >> 3)
    apart = jnp.abs(place(row) - place(col))
    first = jnp.where(apart == 0, CENTRE[0], 0.0)
    for reach, tap in enumerate(TAPS, 1):
        first = jnp.where(apart == reach, tap, first)
    second = jnp.where(apart == 0, CENTRE[1], 0.0)
    mat_ref[...] = jnp.where(col < 2 * NX, first, second).astype(BF16)


def fill_matrix(mat_ref):
    row = lax.broadcasted_iota(jnp.int32, (2 * NY, NY), 0)
    col = lax.broadcasted_iota(jnp.int32, (2 * NY, NY), 1)
    apart = jnp.abs((row & (NY - 1)) - col)
    out = jnp.zeros((2 * NY, NY), F32)
    for reach, tap in enumerate(TAPS, 1):
        out = jnp.where(apart == reach, tap, out)
    mat_ref[...] = out.astype(BF16)


class Rows:
    def __init__(self, *parts):
        self.parts = parts

    def find(self, plane):
        for ref, first, count in self.parts:
            if first <= plane < first + count:
                return ref, plane - first
        raise ValueError(plane)

    def tile(self, plane, j):
        ref, at = self.find(plane)
        return ref[at, j]

    def chunk(self, plane, count):
        ref, at = self.find(plane)
        return ref[pl.ds(at, count)]

    def put(self, plane, j, value):
        ref, at = self.find(plane)
        ref[at, j] = value


def advance(src, prev, dest, vel, first, mat_ref, x_ref, part, inj, see):
    rows = src.chunk(first, 4).reshape(4 * NX, NY)
    high = rows.astype(BF16)
    low = (rows - high.astype(F32)).astype(BF16)
    both = jnp.concatenate([high, low], axis=1)
    along_y = jnp.dot(both, mat_ref[...], preferred_element_type=F32)
    for p in (0, 2):
        sides = []
        for at in (p * NX, (p + 1) * NX):
            sides.append(jnp.concatenate([high[at:at + NX], low[at:at + NX]] * 2, axis=0))
        along_x = jnp.dot(x_ref[...], jnp.concatenate(sides, axis=1), preferred_element_type=F32)
        for q in range(2):
            at = (p + q) * NX
            part[p + q] = (along_y[at:at + NX] + along_x[:, q * NY:(q + 1) * NY]).reshape(8, 8, NY)
    for p in range(4):
        plane = first + p
        for j in range(8):
            here = src.tile(plane, j)
            total = part[p, j]
            for reach, tap in enumerate(TAPS, 1):
                total = total + tap * (src.tile(plane + reach, j) + src.tile(plane - reach, j))
            change = vel.tile(plane, j) * total
            if 4 <= plane < 12:
                change = change + inj[plane - 4, j]
            dest.put(plane, j, (here + here) - prev.tile(plane, j) + change)
            if 0 <= plane < PLANES:
                see(plane, j, change, here)


class Natural:
    def __init__(self, ref, field):
        self.ref, self.field = ref, field

    def tile(self, plane, j):
        return self.ref[pl.ds((self.field * PLANES + plane) * NX + j, 8, stride=8), :]


def half_kernel(*refs, side, field, now_at, prev_at, vel_at, mid_at, masked, ride, send):
    refs = list(refs)
    take = lambda count: [refs.pop(0) for _ in range(count)]
    rows = lambda some, at: Rows(*[(ref, *where) for ref, where in zip(some, at)])
    keep, mat_ref, x_ref, inj = take(4)
    vel = rows(take(len(vel_at)), vel_at)
    now_refs = take(len(now_at))
    prev = Natural(take(1)[0], field) if prev_at is None else rows(take(len(prev_at)), prev_at)
    other_mid = take(max(len(mid_at) - 1, 0))
    if field == 1:
        changes, image_in = take(2)
        del image_in
    take(1)
    out, extra = take(2)
    mid = take(1) if mid_at else []
    message = take(1)[0] if send else None
    part, beyond = refs
    if masked:
        beyond = now_refs[0]
    else:
        inside = keep[...] > 0.0
        for p in range(now_at[0][1]):
            for j in range(8):
                beyond[p, j] = jnp.where(inside, now_refs[0][p, j], 0.0)
    now = rows([beyond, *now_refs[1:]], now_at)
    base = 8 * side
    last = Rows((out, base, 8))
    if mid_at:
        mids = rows([*mid, *other_mid], mid_at)
        starts = range(mid_at[0][0], sum(mid_at[0]), 4)
        seen = [p for p in range(mid_at[0][0], sum(mid_at[0])) if 0 <= p < PLANES]

    def see(first):
        def change_out(plane, j, change, here):
            extra[plane - first, j] = change

        def image_out(plane, j, change, here):
            extra[plane, j] += changes[plane - first, j] * here

        return change_out if field == 0 else image_out

    run = functools.partial(advance, vel=vel, mat_ref=mat_ref, x_ref=x_ref)
    skip = 0
    if mid_at:
        for n, lo in enumerate(starts):
            run(now, prev, mids, first=lo, part=part.at[n % 2], inj=inj.at[0], see=see(seen[0]))
        now, prev, skip = mids, now, len(seen)
    for n, lo in enumerate((base, base + 4)):
        run(now, prev, last, first=lo, part=part.at[n % 2], inj=inj.at[1 if mid_at else 0], see=see(base - skip))
    border = 12 if side else 0
    for p in range(4):
        for j in range(8):
            if ride:
                out[8 + p, j] = vel.tile(border + p, j)
            if send:
                message[p, j] = out[border - base + p, j]


def edge_kernel(keep, message, out):
    inside = keep[...] > 0.0
    for p in range(4):
        for j in range(8):
            out[p, j] = jnp.where(inside, message[8 + p, j], 0.0)


def pack_kernel(now_in, up_msg, down_msg, low_0, high_0, low_1, high_1, mat_ref, x_ref):
    fill_matrix(mat_ref)
    fill_x_matrix(x_ref)
    for field, (low, high) in enumerate(((low_0, high_0), (low_1, high_1))):
        now = Natural(now_in, field)
        for p in range(PLANES):
            for j in range(8):
                tile = now.tile(p, j)
                (high if p >= 8 else low)[p % 8, j] = tile
                if p < 4:
                    down_msg[field, p, j] = tile
                if p >= 12:
                    up_msg[field, p - 12, j] = tile


def spread_kernel(own, out, factor):
    speed = own[...]
    factor[...] = (-2.0 / (16 * STEPS)) / (speed * speed * speed)
    for shot in range(16):
        out[pl.ds(shot * 64, 64), :] = own[...]


def dense(cells, amps, step, steps):
    count = cells.shape[1]
    cell = cells[...]
    z, x, y = cell >> 13, (cell >> 7) & (NX - 1), cell & (NY - 1)
    row = (z - 4) * NX + (x & 7) * 8 + (x >> 3)
    hit = (lax.broadcasted_iota(jnp.int32, (8 * NX, count), 0) == row).astype(F32).astype(BF16)
    hits = jnp.concatenate([hit, hit, hit], axis=1)
    lane = lax.broadcasted_iota(jnp.int32, (NY, count), 0) == y
    sides = []
    for at in range(step, step + steps):
        amount = amps[pl.ds(at, 1), :]
        high = amount.astype(BF16).astype(F32)
        rest = amount - high
        middle = rest.astype(BF16).astype(F32)
        low = rest - middle
        sides.append(jnp.concatenate([jnp.where(lane, part, 0.0).astype(BF16) for part in (high, middle, low)], axis=1))
    both = jnp.concatenate(sides, axis=0)
    return lax.dot_general(hits, both, (((1,), (1,)), ((), ())), preferred_element_type=F32)


def inject_kernel(source_cells, source_amps, cells, amps, token, out_0, out_1, *, step, steps):
    del token
    values = dense(cells, amps, step, steps)
    for at in range(steps):
        out_1[at] = values[:, at * NY:(at + 1) * NY].reshape(8, 8, 8, NY)

    def pick(array, row, column):
        spot = (lax.broadcasted_iota(jnp.int32, array.shape, 0) == row) & (lax.broadcasted_iota(jnp.int32, array.shape, 1) == column)
        return jnp.sum(jnp.where(spot, array, 0.0), keepdims=True)

    sub = lax.broadcasted_iota(jnp.int32, (8, NY), 0)
    lane = lax.broadcasted_iota(jnp.int32, (8, NY), 1)
    places = source_cells[...].astype(F32)
    count = source_cells.shape[1]
    rows, columns, amounts = [], [], []
    for n in range(count):
        cell = pick(places, 0, n).astype(jnp.int32)
        z, x, y = cell >> 13, (cell >> 7) & (NX - 1), cell & (NY - 1)
        rows.append(sub - ((z - 4) * NX + (x & 7) * 8 + (x >> 3)))
        columns.append(lane == y)
        amounts.append([pick(source_amps[...], n, step + at) for at in range(steps)])
    for p in range(8):
        for j in range(8):
            hits = [(row == -(p * NX + j * 8)) & column for row, column in zip(rows, columns)]
            for at in range(steps):
                total = jnp.zeros((8, NY), F32)
                for hit, amount in zip(hits, amounts):
                    total = total + jnp.where(hit, amount[at], 0.0)
                out_0[at, p, j] = total


def open_kernel(keep_below, keep_above, gathered, below, above,
                vel, image, below_out_0, above_out_0, below_out_1, above_out_1):
    image[...] = jnp.zeros_like(image)
    for p in range(PLANES):
        for j in range(8):
            line = gathered[pl.ds((j // 4) * 64 + p * 4 + j % 4, 8, stride=128), :]
            vel[p, j] = line * line * (1.0 / SCALE)
    for keep, src, dests in ((keep_below, below, (below_out_0, below_out_1)), (keep_above, above, (above_out_0, above_out_1))):
        inside = keep[...] > 0.0
        for field, dest in enumerate(dests):
            for p in range(4):
                for j in range(8):
                    dest[p, j] = jnp.where(inside, src[field, p, j], 0.0)


def terms_kernel(image, out):
    for p in range(PLANES):
        for j in range(8):
            out[pl.ds((j // 4) * 64 + p * 4 + j % 4, 8, stride=128), :] = image[p, j]


def sum_kernel(terms, factor, out):
    total = terms[0:64, :]
    for shot in range(1, 16):
        total = total + terms[pl.ds(64 * shot, 64), :]
    out[...] = total * factor[...]


def close_kernel(before_low_0, before_high_0, low_0, high_0, before_low_1, before_high_1, low_1, high_1, before, after):
    for field, (before_low, before_high, low, high) in enumerate(
            ((before_low_0, before_high_0, low_0, high_0), (before_low_1, before_high_1, low_1, high_1))):
        for p in range(PLANES):
            for j in range(8):
                rows = pl.ds((field * PLANES + p) * NX + j, 8, stride=8)
                before[rows, :] = (before_high if p >= 8 else before_low)[p % 8, j]
                after[rows, :] = (high if p >= 8 else low)[p % 8, j]


def tiles(*lead):
    return jax.ShapeDtypeStruct((*lead, 8, 8, NY), F32)


def rows_of(count):
    return jax.ShapeDtypeStruct((count, NY), F32)


def call(kernel, args, outs, flops, scratch=(), aliases=None):
    whole = pl.BlockSpec(memory_space=pltpu.VMEM)
    return pl.pallas_call(
        kernel,
        in_specs=[whole] * len(args),
        out_specs=jax.tree.map(lambda _: whole, outs),
        out_shape=outs,
        scratch_shapes=list(scratch),
        input_output_aliases=aliases or {},
        compiler_params=pltpu.CompilerParams(vmem_limit_bytes=VMEM_LIMIT),
        cost_estimate=pl.CostEstimate(flops=flops, bytes_accessed=1 << 20, transcendentals=0),
    )(*args)


def body(
    velocity, fields_prev, fields_now, source_cells, source_traces, receiver_cells, receiver_traces
):
    slabs, shots = lax.axis_size("slab"), lax.axis_size("shot")
    up = [(i, (i + 1) % slabs) for i in range(slabs)]
    down = [(j, i) for i, j in up]
    slab = lax.axis_index("slab")
    keep = [jnp.full((8, NY), slab > 0, F32), jnp.full((8, NY), slab < slabs - 1, F32)]

    vel_rows = velocity.reshape(PLANES * 4, NY)
    spread, factor = call(spread_kernel, (vel_rows,), (rows_of(shots * 64), rows_of(64)), 1 << 20)
    gathered = lax.all_to_all(spread.reshape(shots, 64, NY), "shot", 0, 0, tiled=True)
    half, quarter = tiles(8), tiles(4)
    mat, mat_x = jax.ShapeDtypeStruct((2 * NY, NY), BF16), jax.ShapeDtypeStruct((NX, 4 * NX), BF16)
    up_msg, down_msg, low_0, high_0, low_1, high_1, mat, mat_x = call(
        pack_kernel, (fields_now.reshape(-1, NY),), (*[tiles(2, 4)] * 2, *[half] * 4, mat, mat_x), 1 << 22)
    now = [[low_0, high_0], [low_1, high_1]]
    arrived = [lax.ppermute(up_msg, "slab", up), lax.ppermute(down_msg, "slab", down)]
    marks = (source_cells, source_traces[0].T, receiver_cells, receiver_traces[0])
    vel, image, *far = call(
        open_kernel, (*keep, gathered.reshape(shots * 64, NY), *arrived), (tiles(16), tiles(16), *[quarter] * 4), 1 << 22)
    beyond = [far[:2], far[2:]]
    vels = [[(vel, (0, 16))], [(vel, (0, 16))]]
    prev_rows = fields_prev.reshape(-1, NY)

    lengths = (1, 2, 2, 2, 1)
    token, step, prev = image, 0, None
    for block, length in enumerate(lengths):
        final = block == len(lengths) - 1
        to_send = 0 if final else 4 * lengths[block + 1]
        order = (1, 0) if block % 2 == 0 else (0, 1)
        first = block == 0
        news, mids, sent = ([[None, None], [None, None]] for _ in range(3))
        changes = [None, None]
        inj = call(functools.partial(inject_kernel, step=step, steps=length),
                   (*marks, mat if block == 0 else token), (tiles(length, 8), tiles(length, 8)), 1 << 24)
        walk = [(f, n) for f in range(2) for n in range(2)] if length == 2 or final else [(f, n) for n in range(2) for f in range(2)]
        for field, n in walk:
            if True:
                side = order[n]
                if block == 1 and field == 0:
                    edge = call(edge_kernel, (keep[side], beyond[0][side]), quarter, 1 << 16)
                    vels[side] = [(vel, (0, 16)), (edge, (16 if side else -4, 4))]
                reach = 4 * length
                now_list = [(beyond[field][side], (16 if side else -reach, reach)), (now[field][0], (0, 8)), (now[field][1], (8, 8))]
                prev_list = [(prev_rows, None)] if first else prev[field]
                mid_list = []
                if length == 2:
                    mid_at = (4, 16) if side and n == 0 else (-4, 16) if n == 0 else (12, 8) if side else (-4, 8)
                    mid_list = [(None, mid_at)] + ([mids[field][order[0]]] if n == 1 else [])
                args = [keep[side], mat, mat_x, inj[field]] + [a for a, _ in vels[side]]
                args += [a for a, _ in now_list] + [a for a, _ in prev_list] + [a for a, _ in mid_list[1:]]
                aliases = {}
                if field == 1:
                    args += [changes[side], image]
                    aliases = {len(args) - 1: 1}
                args.append(token)
                seen = (12 if n == 0 else 4) if length == 2 else 0
                ride = first and field == 0
                send = to_send == 4
                outs = [tiles(12) if ride else half, tiles(seen + 8) if field == 0 else tiles(16)]
                if length == 2:
                    outs.append(tiles(mid_at[1]))
                if send:
                    outs.append(quarter)
                out, extra, *rest = call(
                    functools.partial(
                        half_kernel, side=side, field=field, now_at=[at for _, at in now_list],
                        prev_at=None if first else [at for _, at in prev_list], vel_at=[at for _, at in vels[side]],
                        mid_at=[at for _, at in mid_list], masked=first, ride=ride, send=send),
                    args, outs, 1 << 25,
                    scratch=(pltpu.VMEM((2, 4, 8, 8, NY), F32), pltpu.VMEM((8, 8, 8, NY), F32)), aliases=aliases)
                token = out
                news[field][side] = out
                if length == 2:
                    mids[field][side] = (rest[0], mid_at)
                if field == 0:
                    changes[side] = extra
                else:
                    image = extra
                if not final:
                    sent[field][1 - side] = lax.ppermute(rest[-1] if send else out, "slab", up if side else down)
        if first:
            prev = [[(a, (0, 8)), (b, (8, 8)), (beyond[f][0], (-4, 4)), (beyond[f][1], (16, 4))] for f, (a, b) in enumerate(now)]
        else:
            prev = mids
        before_last, now, beyond = now, news, sent
        step += length

    terms = call(terms_kernel, (image,), rows_of(shots * 64), 1 << 20)
    terms = lax.all_to_all(terms.reshape(shots, 64, NY), "shot", 0, 0, tiled=True)
    args = []
    for field in range(2):
        args += [*before_last[field], *now[field]]
    before, after = call(close_kernel, args, (rows_of(2 * PLANES * NX), rows_of(2 * PLANES * NX)), 1 << 22)
    gradient = call(sum_kernel, (terms.reshape(shots * 64, NY), factor), rows_of(64), 1 << 18).reshape(velocity.shape)
    shape = fields_now.shape
    return gradient, before.reshape(shape), after.reshape(shape)


def solution(mesh):
    return jax.shard_map(
        body,
        mesh=mesh,
        in_specs=(
            P("slab", "shot", None),
            P("shot", None, "slab", None, None),
            P("shot", None, "slab", None, None),
            P("shot", "slab"),
            P("shot", None, "slab"),
            P("shot", "slab"),
            P("shot", None, "slab"),
        ),
        out_specs=(
            P("slab", "shot", None),
            P("shot", None, "slab", None, None),
            P("shot", None, "slab", None, None),
        ),
        check_vma=False,
    )
```
